256 devices in a mesh: space: 16 (over y, x), tblock: 16 (over z, core).
Axes of the slice: x: 4, y: 4, z: 8, core: 2. Of those that a mesh axis runs over, the one named last changes fastest.
Arguments:
- snapshots: bfloat16 [16, 256, 3, 106496], P('tblock', None, None, 'space'), may hold values from -70 to 70
Outputs:
- modes: bfloat16 [128, 2, 4, 3, 106496], P('tblock', None, None, None, 'space')
- energies: float32 [128, 4], P('tblock')
The draws below stay inside these ranges and needn't reach their ends.
All inputs are finite; a program needn't handle non-finite values.
Results may differ from the reference program's by a relative error of at most 0.0085.
Values may be sent and summed in bfloat16 or wider, within the bound.
A program may use at most 128 MiB of HBM per device.

```python
import math
import jax
import jax.numpy as jnp
from jax import lax

STEPS = 256
FREQS = 128
BLOCKS = 16
POINTS = 106496
MODES = 4
SUBSPACE_ITERS = 6


def draw_snapshots(key, part):
    key = jax.random.fold_in(key, 11)
    keys = jax.random.split(key, 4)
    amp = jnp.exp(jax.random.uniform(keys[0], (BLOCKS, 1, 1, 1), jnp.float32, math.log(0.6), math.log(1.8)))
    place = jnp.arange(POINTS, dtype=jnp.float32) / POINTS
    ramp = jnp.exp(math.log(3.0) * place)[None, None, None, :]
    rough = jax.random.uniform(keys[1], (1, 1, 3, POINTS), jnp.float32, 0.5, 1.5)
    shared = jnp.clip(jax.random.normal(keys[2], (1, STEPS, 3, POINTS), jnp.float32), -4.0, 4.0)
    noise = jnp.clip(jax.random.normal(keys[3], (BLOCKS, STEPS, 3, POINTS), jnp.float32), -4.0, 4.0)
    values = amp * ramp * rough * (0.8 * shared + noise)
    return values.astype(jnp.bfloat16)


def setup_inputs(seed: int = 0) -> dict:
    key_list = jax.random.split(jax.random.key(seed), 2)
    snapshots = draw_snapshots(jax.random.fold_in(key_list[1], 71), 0)
    return {"snapshots": snapshots}


def spectral_table(step_count):
    times = jnp.arange(step_count, dtype=jnp.int32)
    orders = jnp.arange(1, step_count // 2 + 1, dtype=jnp.int32)
    phase = orders[:, None] * times[None, :] % step_count
    angle = 2.0 * math.pi / step_count * phase.astype(jnp.float32)
    window = 0.5 - 0.5 * jnp.cos(2.0 * math.pi / step_count * times.astype(jnp.float32))
    scaled = window / math.sqrt(0.375 * step_count)
    rows = jnp.stack([scaled * jnp.cos(angle), -scaled * jnp.sin(angle)], axis=1)
    return rows.reshape(step_count, step_count).astype(jnp.bfloat16)

def batch_mult(left, right):
    return jnp.einsum('fbe,fek->fbk', left, right, precision=lax.Precision.HIGHEST)

def apply_gram(gram_real, gram_imag, vec_real, vec_imag):
    out_real = batch_mult(gram_real, vec_real) - batch_mult(gram_imag, vec_imag)
    out_imag = batch_mult(gram_real, vec_imag) + batch_mult(gram_imag, vec_real)
    return (out_real, out_imag)

def orthonormal(wide_real, wide_imag):
    done_real = []
    done_imag = []
    for column in range(wide_real.shape[2]):
        vec_real = wide_real[:, :, column]
        vec_imag = wide_imag[:, :, column]
        for earlier in range(column):
            base_real = done_real[earlier]
            base_imag = done_imag[earlier]
            proj_real = lax.optimization_barrier(jnp.sum(base_real * vec_real + base_imag * vec_imag, axis=1, keepdims=True))
            proj_imag = lax.optimization_barrier(jnp.sum(base_real * vec_imag - base_imag * vec_real, axis=1, keepdims=True))
            vec_real = vec_real - (base_real * proj_real - base_imag * proj_imag)
            vec_imag = vec_imag - (base_real * proj_imag + base_imag * proj_real)
        length = jnp.sqrt(lax.optimization_barrier(jnp.sum(vec_real * vec_real + vec_imag * vec_imag, axis=1, keepdims=True)))
        done_real.append(vec_real / length)
        done_imag.append(vec_imag / length)
    return (jnp.stack(done_real, axis=2), jnp.stack(done_imag, axis=2))

def leading_modes(gram_real, gram_imag):
    freq_count, block_count = (gram_real.shape[0], gram_real.shape[1])
    basis = jnp.eye(block_count, MODES, dtype=jnp.float32)
    vec_real = jnp.broadcast_to(basis[None], (freq_count, block_count, MODES))
    vec_imag = jnp.zeros((freq_count, block_count, MODES), jnp.float32)
    for sweep in range(SUBSPACE_ITERS):
        wide_real, wide_imag = apply_gram(gram_real, gram_imag, vec_real, vec_imag)
        vec_real, vec_imag = orthonormal(wide_real, wide_imag)
    wide_real, wide_imag = apply_gram(gram_real, gram_imag, vec_real, vec_imag)
    energy = lax.optimization_barrier(jnp.sum(vec_real * wide_real + vec_imag * wide_imag, axis=1))
    scale = 1.0 / jnp.sqrt(energy)
    amp_real = jnp.transpose(vec_real, (0, 2, 1)) * scale[:, :, None]
    amp_imag = jnp.transpose(vec_imag, (0, 2, 1)) * scale[:, :, None]
    first = jnp.stack([amp_real, -amp_imag], axis=2)
    second = jnp.stack([amp_imag, amp_real], axis=2)
    coef = jnp.stack([first, second], axis=1).astype(jnp.bfloat16)
    return (coef, energy)

def reference(snapshots):
    dft_table = spectral_table(STEPS).astype(jnp.float32)

    def transform(block):
        series = block.reshape(STEPS, 3 * POINTS).astype(jnp.float32)
        return jnp.dot(dft_table, series, precision=lax.Precision.HIGHEST).astype(jnp.bfloat16)
    spectra = lax.map(transform, snapshots)
    bins = jnp.arange(FREQS, dtype=jnp.int32)

    def bin_rows(index):
        rows = lax.dynamic_slice_in_dim(spectra, (2 * index).astype(jnp.int32), 2, 1)
        return jnp.transpose(rows, (1, 0, 2)).astype(jnp.float32)

    def bin_products(index):
        rows = bin_rows(index)
        return jnp.einsum('rbx,sex->rsbe', rows, rows, precision=lax.Precision.HIGHEST)
    products = lax.map(bin_products, bins) / (3.0 * POINTS)
    gram_real = products[:, 0, 0] + products[:, 1, 1]
    gram_imag = products[:, 0, 1] - products[:, 1, 0]
    coef, energies = leading_modes(gram_real, gram_imag)

    def bin_modes(pair):
        index, weights = pair
        rows = bin_rows(index)
        return jnp.einsum('ojrb,rbx->ojx', weights.astype(jnp.float32), rows, precision=lax.Precision.HIGHEST).astype(jnp.bfloat16)
    modes = lax.map(bin_modes, (bins, coef))
    return (modes.reshape(FREQS, 2, MODES, 3, POINTS), energies)
```

```python
import functools
import math

import jax
import jax.numpy as jnp
import numpy as np
from jax import lax
from jax.experimental import pallas as pl
from jax.experimental.pallas import tpu as pltpu
from jax.sharding import PartitionSpec as P

MODES = 4
SUBSPACE_ITERS = 6
BLOCKS = 16
STEPS = 256
BINS = 8
ROWS = 2 * BINS
COMPS = 3
CUTS = 4
LANES = 128
MESH = pl.DeviceIdType.MESH
VMEM_BYTES = 56 * 2**20


def spectral_table():
    times = np.arange(STEPS, dtype=np.int32)
    orders = np.arange(1, STEPS // 2 + 1, dtype=np.int32)
    phase = orders[:, None] * times[None, :] % STEPS
    angle = np.float32(2.0 * math.pi / STEPS) * phase.astype(np.float32)
    swing = np.cos(np.float32(2.0 * math.pi / STEPS) * times.astype(np.float32))
    window = np.float32(0.5) - np.float32(0.5) * swing
    scaled = window / np.float32(math.sqrt(0.375 * STEPS))
    rows = np.stack([scaled * np.cos(angle), -scaled * np.sin(angle)], axis=1)
    return jnp.asarray(rows.reshape(STEPS, STEPS).astype(np.float32)).astype(jnp.bfloat16)


def pack_gram(total):
    width = total.shape[1]
    cube = total.reshape(BLOCKS, ROWS, width)
    row = lax.broadcasted_iota(jnp.int32, (ROWS, width), 0)
    lane = lax.broadcasted_iota(jnp.int32, (ROWS, width), 1) % ROWS
    same_bin = row // 2 == lane // 2
    same_part = row % 2 == lane % 2
    first = jnp.where(same_bin & same_part, 1.0, 0.0)
    other = jnp.where(same_bin & (row % 2 < lane % 2), 1.0, 0.0)
    other = jnp.where(same_bin & (row % 2 > lane % 2), -1.0, other)
    real = jnp.sum(cube * first[None], axis=1)
    imag = jnp.sum(cube * other[None], axis=1)
    even = lax.broadcasted_iota(jnp.int32, (BLOCKS, width), 1) % 2 == 0
    real = real + pltpu.roll(real, width - 1, 1)
    imag = imag + pltpu.roll(imag, 1, 1)
    return jnp.where(even, real, imag)


def column_sum(value):
    return jnp.sum(value, axis=0, keepdims=True)


def leading_modes(packed, gram_ref):
    even = lax.broadcasted_iota(jnp.int32, (BLOCKS, LANES), 1) % 2 == 0
    per_half = LANES // ROWS
    for half in range(2):
        part = packed[:, half * LANES : (half + 1) * LANES]
        real = jnp.where(even, part, pltpu.roll(part, 1, 1))
        imag = jnp.where(even, pltpu.roll(part, LANES - 1, 1), part)
        for near in range(per_half):
            shift = (LANES - ROWS * near) % LANES
            block = half * per_half + near
            gram_ref[0, block] = real if shift == 0 else pltpu.roll(real, shift, 1)
            gram_ref[1, block] = imag if shift == 0 else pltpu.roll(imag, shift, 1)

    def apply_gram(vec_real, vec_imag):
        out_real = [None] * MODES
        out_imag = [None] * MODES
        for block in range(BLOCKS):
            real = gram_ref[0, block]
            imag = gram_ref[1, block]
            for j in range(MODES):
                row_real = vec_real[j][block : block + 1]
                row_imag = vec_imag[j][block : block + 1]
                term_real = real * row_real - imag * row_imag
                term_imag = real * row_imag + imag * row_real
                out_real[j] = term_real if block == 0 else out_real[j] + term_real
                out_imag[j] = term_imag if block == 0 else out_imag[j] + term_imag
        return out_real, out_imag

    def orthonormal(vec_real, vec_imag):
        vec_real = list(vec_real)
        vec_imag = list(vec_imag)
        for i in range(MODES):
            base_real = vec_real[i]
            base_imag = vec_imag[i]
            square = column_sum(base_real * base_real + base_imag * base_imag)
            inverse = 1.0 / square
            for j in range(i + 1, MODES):
                proj_real = column_sum(base_real * vec_real[j] + base_imag * vec_imag[j]) * inverse
                proj_imag = column_sum(base_real * vec_imag[j] - base_imag * vec_real[j]) * inverse
                vec_real[j] = vec_real[j] - (base_real * proj_real - base_imag * proj_imag)
                vec_imag[j] = vec_imag[j] - (base_real * proj_imag + base_imag * proj_real)
            scale = lax.rsqrt(square)
            vec_real[i] = base_real * scale
            vec_imag[i] = base_imag * scale
        return vec_real, vec_imag

    wide_real = [gram_ref[0, j] for j in range(MODES)]
    wide_imag = [gram_ref[1, j] for j in range(MODES)]
    vec_real, vec_imag = orthonormal(wide_real, wide_imag)

    def sweep(_, carry):
        return orthonormal(*apply_gram(*carry))

    vec_real, vec_imag = lax.fori_loop(1, SUBSPACE_ITERS, sweep, (vec_real, vec_imag))
    wide_real, wide_imag = apply_gram(vec_real, vec_imag)
    energies = [
        column_sum(vec_real[j] * wide_real[j] + vec_imag[j] * wide_imag[j]) for j in range(MODES)
    ]
    return vec_real, vec_imag, energies


def coefficient_matrix(vec_real, vec_imag, energies, order_ref):
    lane = lax.broadcasted_iota(jnp.int32, (BLOCKS, LANES), 1)
    even = lane % 2 == 0
    first = jnp.zeros((BLOCKS, LANES), jnp.float32)
    second = jnp.zeros((BLOCKS, LANES), jnp.float32)
    for j in range(MODES):
        scale = 1.0 / jnp.sqrt(energies[j])
        amp_real = vec_real[j] * scale
        amp_imag = vec_imag[j] * scale
        on_real = jnp.where(even, amp_real, amp_imag)
        on_imag = jnp.where(even, -amp_imag, amp_real)
        if j:
            on_real = pltpu.roll(on_real, ROWS * j, 1)
            on_imag = pltpu.roll(on_imag, ROWS * j, 1)
        here = lane // ROWS == j
        first = jnp.where(here, on_real, first)
        second = jnp.where(here, on_imag, second)
    shape = (BLOCKS, ROWS, LANES)
    row = lax.broadcasted_iota(jnp.int32, shape, 1)
    column = lax.broadcasted_iota(jnp.int32, shape, 2)
    whole = jnp.where(
        row % 2 == 0,
        jnp.broadcast_to(first[:, None, :], shape),
        jnp.broadcast_to(second[:, None, :], shape),
    )
    whole = jnp.where(row // 2 == column % ROWS // 2, whole, 0.0)
    turned = whole.reshape(BLOCKS * ROWS, LANES).T
    for j in range(MODES):
        for half in range(2):
            piece = turned[ROWS * j : ROWS * (j + 1), half * LANES : (half + 1) * LANES]
            order_ref[half, pl.ds(j, ROWS, stride=MODES), :] = piece
    return jnp.concatenate([order_ref[0], order_ref[1]], axis=1).astype(jnp.bfloat16)


def spectra_kernel(
    cut,
    scale,
    table_ref,
    series_ref,
    mine_ref,
    coef_ref,
    energy_ref,
    taken_ref,
    made_ref,
    total_ref,
    packed_ref,
    gram_ref,
    order_ref,
    take_sem,
    send_sem,
    recv_sem,
    sum_send_sem,
    sum_recv_sem,
):
    chunks = COMPS * CUTS
    here = lax.axis_index("space")
    me = lax.axis_index("tblock")
    level = me // 2
    core = lax.rem(me, 2)

    def peer(dz, dc):
        return lax.rem(level + dz, 8) * 2 + lax.rem(core + dc, 2)

    peers = [(dz, dc) for dz in (4, 3, 5, 2, 6, 1, 7, 0) for dc in (0, 1)][:-2] + [(0, 1)]

    barrier = pltpu.get_barrier_semaphore()
    for dz, dc in peers:
        pl.semaphore_signal(barrier, inc=1, device_id={"tblock": peer(dz, dc)}, device_id_type=MESH)
    for d in range(1, 16):
        pl.semaphore_signal(
            barrier, inc=1, device_id={"space": lax.rem(here + d, 16)}, device_id_type=MESH
        )

    def take(k):
        comp = k // CUTS
        start = pl.multiple_of(lax.rem(k, CUTS) * cut, LANES)
        slot = lax.rem(k, 2)
        return pltpu.make_async_copy(
            series_ref.at[comp, :, pl.ds(start, cut)], taken_ref.at[slot], take_sem.at[slot]
        )

    def send(k, dz, dc):
        to = peer(dz, dc)
        return pltpu.make_async_remote_copy(
            src_ref=made_ref.at[k, to],
            dst_ref=mine_ref.at[k, me],
            send_sem=send_sem.at[k, to],
            recv_sem=recv_sem.at[k, me],
            device_id={"tblock": to},
            device_id_type=MESH,
        )

    def arrival(k, dz, dc):
        sender = peer(dz, dc)
        return pltpu.make_async_remote_copy(
            src_ref=made_ref.at[k, sender],
            dst_ref=mine_ref.at[k, sender],
            send_sem=send_sem.at[k, sender],
            recv_sem=recv_sem.at[k, sender],
            device_id={"tblock": sender},
            device_id_type=MESH,
        )

    def make(k):
        take(k).wait()
        spectra = jnp.dot(
            table_ref[...], taken_ref[lax.rem(k, 2)], preferred_element_type=jnp.float32
        )
        made_ref[k] = spectra.astype(jnp.bfloat16).reshape(BLOCKS, ROWS, cut)
        mine_ref[k, me] = made_ref[k, me]

    take(0).start()
    take(1).start()
    make(0)
    pl.semaphore_wait(barrier, 30)
    for dz, dc in peers:
        send(0, dz, dc).start()

    def make_and_send(k, carry):
        @pl.when(k + 1 < chunks)
        def _():
            take(k + 1).start()

        make(k)
        for dz, dc in peers:
            send(k, dz, dc).start()
        return carry

    lax.fori_loop(1, chunks, make_and_send, 0)

    total_ref[...] = jnp.zeros_like(total_ref)

    def gather(k, carry):
        for dz, dc in peers:
            arrival(k, dz, dc).wait_recv()
        rows = mine_ref[k].reshape(BLOCKS * ROWS, cut)
        total_ref[...] += lax.dot_general(
            rows, rows, (((1,), (1,)), ((), ())), preferred_element_type=jnp.float32
        )
        return carry

    lax.fori_loop(0, chunks, gather, 0)

    packed_ref[here] = pack_gram(total_ref[...])

    def exchange(d, arriving):
        other = lax.rem(here + d, 16)
        slot = other if arriving else here
        return pltpu.make_async_remote_copy(
            src_ref=packed_ref.at[here],
            dst_ref=packed_ref.at[slot],
            send_sem=sum_send_sem.at[other],
            recv_sem=sum_recv_sem.at[slot],
            device_id={"space": other},
            device_id_type=MESH,
        )

    for d in range(1, 16):
        exchange(d, False).start()
    for d in range(1, 16):
        exchange(d, True).wait_recv()
    packed = packed_ref[0]
    for s in range(1, 16):
        packed = packed + packed_ref[s]
    packed = packed / scale

    vec_real, vec_imag, energies = leading_modes(packed, gram_ref)
    coef_ref[...] = coefficient_matrix(vec_real, vec_imag, energies, order_ref)
    wide = jnp.concatenate(energies, axis=0)
    lane = lax.broadcasted_iota(jnp.int32, (MODES, LANES), 1)
    narrow = wide
    for f in range(1, BINS):
        narrow = jnp.where(lane == f, pltpu.roll(wide, LANES - f, 1), narrow)
    energy_ref[...] = narrow[:, :BINS]

    def finish(k, carry):
        for dz, dc in peers:
            send(k, dz, dc).wait_send()
        return carry

    lax.fori_loop(0, chunks, finish, 0)
    for d in range(1, 16):
        exchange(d, False).wait_send()


def modes_kernel(coef_ref, mine_ref, out_ref):
    k = pl.program_id(0)
    rows = mine_ref[k].reshape(BLOCKS * ROWS, mine_ref.shape[3])
    modes = jnp.dot(coef_ref[...], rows, preferred_element_type=jnp.float32)
    modes = modes.astype(jnp.bfloat16)
    for f in range(BINS):
        for part in range(2):
            start = (f * 2 + part) * MODES
            out_ref[f, part, 0] = modes[start : start + MODES]


def local(snapshots, space_count):
    points = snapshots.shape[3]
    cut = points // CUTS
    chunks = COMPS * CUTS
    series = jnp.transpose(snapshots, (0, 2, 1, 3)).reshape(COMPS, STEPS, points)
    vmem = pl.BlockSpec(memory_space=pltpu.VMEM)
    mine, coef, energies = pl.pallas_call(
        functools.partial(spectra_kernel, cut, float(COMPS * points * space_count)),
        out_shape=(
            jax.ShapeDtypeStruct((chunks, BLOCKS, ROWS, cut), jnp.bfloat16),
            jax.ShapeDtypeStruct((BINS * 2 * MODES, BLOCKS * ROWS), jnp.bfloat16),
            jax.ShapeDtypeStruct((MODES, BINS), jnp.float32),
        ),
        in_specs=[vmem, pl.BlockSpec(memory_space=pl.ANY)],
        out_specs=(vmem, vmem, vmem),
        scratch_shapes=[
            pltpu.VMEM((2, STEPS, cut), jnp.bfloat16),
            pltpu.VMEM((chunks, BLOCKS, ROWS, cut), jnp.bfloat16),
            pltpu.VMEM((BLOCKS * ROWS, BLOCKS * ROWS), jnp.float32),
            pltpu.VMEM((16, BLOCKS, BLOCKS * ROWS), jnp.float32),
            pltpu.VMEM((2, BLOCKS, BLOCKS, LANES), jnp.float32),
            pltpu.VMEM((2, BINS * 2 * MODES, LANES), jnp.float32),
            pltpu.SemaphoreType.DMA((2,)),
            pltpu.SemaphoreType.DMA((chunks, 16)),
            pltpu.SemaphoreType.DMA((chunks, 16)),
            pltpu.SemaphoreType.DMA((16,)),
            pltpu.SemaphoreType.DMA((16,)),
        ],
        compiler_params=pltpu.CompilerParams(
            collective_id=0, has_side_effects=True, vmem_limit_bytes=VMEM_BYTES
        ),
        cost_estimate=pl.CostEstimate(
            flops=4 * STEPS * STEPS * COMPS * points,
            bytes_accessed=2 * STEPS * COMPS * points,
            transcendentals=0,
        ),
        name="spectra_exchange",
    )(spectral_table(), series)
    modes = pl.pallas_call(
        modes_kernel,
        grid=(chunks,),
        out_shape=jax.ShapeDtypeStruct((BINS, 2, COMPS, MODES, points), jnp.bfloat16),
        in_specs=[vmem, vmem],
        out_specs=pl.BlockSpec(
            (BINS, 2, 1, MODES, cut), lambda k: (0, 0, k // CUTS, 0, lax.rem(k, CUTS))
        ),
        compiler_params=pltpu.CompilerParams(vmem_limit_bytes=VMEM_BYTES),
        cost_estimate=pl.CostEstimate(
            flops=4 * STEPS * BINS * 2 * MODES * COMPS * points,
            bytes_accessed=2 * STEPS * COMPS * points,
            transcendentals=0,
        ),
        name="modes_product",
    )(coef, mine)
    return jnp.transpose(modes, (0, 1, 3, 2, 4)), energies.T


def solution(mesh):
    in_specs = (P("tblock", None, None, "space"),)
    out_specs = (P("tblock", None, None, None, "space"), P("tblock", None))
    body = functools.partial(local, space_count=mesh.shape["space"])
    return jax.shard_map(body, mesh=mesh, in_specs=in_specs, out_specs=out_specs, check_vma=False)
```

```python
import functools
import math

import jax
import jax.numpy as jnp
import numpy as np
from jax import lax
from jax.experimental import pallas as pl
from jax.experimental.pallas import tpu as pltpu
from jax.sharding import PartitionSpec as P

MODES = 4
SUBSPACE_ITERS = 6
BLOCKS = 16
STEPS = 256
BINS = 8
ROWS = 2 * BINS
COMPS = 3
CUTS = 4
LANES = 128
MESH = pl.DeviceIdType.MESH
VMEM_BYTES = 44 * 2**20


def spectral_table():
    times = np.arange(STEPS, dtype=np.int32)
    orders = np.arange(1, STEPS // 2 + 1, dtype=np.int32)
    phase = orders[:, None] * times[None, :] % STEPS
    angle = np.float32(2.0 * math.pi / STEPS) * phase.astype(np.float32)
    swing = np.cos(np.float32(2.0 * math.pi / STEPS) * times.astype(np.float32))
    window = np.float32(0.5) - np.float32(0.5) * swing
    scaled = window / np.float32(math.sqrt(0.375 * STEPS))
    rows = np.stack([scaled * np.cos(angle), -scaled * np.sin(angle)], axis=1)
    return jnp.asarray(rows.reshape(STEPS, STEPS).astype(np.float32))


def pack_gram(total):
    width = total.shape[1]
    cube = total.reshape(BLOCKS, ROWS, width)
    row = lax.broadcasted_iota(jnp.int32, (ROWS, width), 0)
    lane = lax.broadcasted_iota(jnp.int32, (ROWS, width), 1) % ROWS
    same_bin = row // 2 == lane // 2
    same_part = row % 2 == lane % 2
    first = jnp.where(same_bin & same_part, 1.0, 0.0)
    other = jnp.where(same_bin & (row % 2 < lane % 2), 1.0, 0.0)
    other = jnp.where(same_bin & (row % 2 > lane % 2), -1.0, other)
    real = jnp.sum(cube * first[None], axis=1)
    imag = jnp.sum(cube * other[None], axis=1)
    even = lax.broadcasted_iota(jnp.int32, (BLOCKS, width), 1) % 2 == 0
    real = real + pltpu.roll(real, width - 1, 1)
    imag = imag + pltpu.roll(imag, 1, 1)
    return jnp.where(even, real, imag)


def column_sum(value):
    return jnp.sum(value, axis=0, keepdims=True)


def leading_modes(packed, gram_ref):
    even = lax.broadcasted_iota(jnp.int32, (BLOCKS, LANES), 1) % 2 == 0
    per_half = LANES // ROWS
    for half in range(2):
        part = packed[:, half * LANES : (half + 1) * LANES]
        real = jnp.where(even, part, pltpu.roll(part, 1, 1))
        imag = jnp.where(even, pltpu.roll(part, LANES - 1, 1), part)
        for near in range(per_half):
            shift = (LANES - ROWS * near) % LANES
            block = half * per_half + near
            gram_ref[0, block] = real if shift == 0 else pltpu.roll(real, shift, 1)
            gram_ref[1, block] = imag if shift == 0 else pltpu.roll(imag, shift, 1)

    def apply_gram(vec_real, vec_imag):
        out_real = [None] * MODES
        out_imag = [None] * MODES
        for block in range(BLOCKS):
            real = gram_ref[0, block]
            imag = gram_ref[1, block]
            for j in range(MODES):
                row_real = vec_real[j][block : block + 1]
                row_imag = vec_imag[j][block : block + 1]
                term_real = real * row_real - imag * row_imag
                term_imag = real * row_imag + imag * row_real
                out_real[j] = term_real if block == 0 else out_real[j] + term_real
                out_imag[j] = term_imag if block == 0 else out_imag[j] + term_imag
        return out_real, out_imag

    def orthonormal(vec_real, vec_imag):
        vec_real = list(vec_real)
        vec_imag = list(vec_imag)
        for i in range(MODES):
            base_real = vec_real[i]
            base_imag = vec_imag[i]
            square = column_sum(base_real * base_real + base_imag * base_imag)
            inverse = 1.0 / square
            for j in range(i + 1, MODES):
                proj_real = column_sum(base_real * vec_real[j] + base_imag * vec_imag[j]) * inverse
                proj_imag = column_sum(base_real * vec_imag[j] - base_imag * vec_real[j]) * inverse
                vec_real[j] = vec_real[j] - (base_real * proj_real - base_imag * proj_imag)
                vec_imag[j] = vec_imag[j] - (base_real * proj_imag + base_imag * proj_real)
            scale = lax.rsqrt(square)
            vec_real[i] = base_real * scale
            vec_imag[i] = base_imag * scale
        return vec_real, vec_imag

    wide_real = [gram_ref[0, j] for j in range(MODES)]
    wide_imag = [gram_ref[1, j] for j in range(MODES)]
    vec_real, vec_imag = orthonormal(wide_real, wide_imag)

    def sweep(_, carry):
        return orthonormal(*apply_gram(*carry))

    vec_real, vec_imag = lax.fori_loop(1, SUBSPACE_ITERS, sweep, (vec_real, vec_imag))
    wide_real, wide_imag = apply_gram(vec_real, vec_imag)
    energies = [
        column_sum(vec_real[j] * wide_real[j] + vec_imag[j] * wide_imag[j]) for j in range(MODES)
    ]
    return vec_real, vec_imag, energies


def coefficient_matrix(vec_real, vec_imag, energies, order_ref):
    lane = lax.broadcasted_iota(jnp.int32, (BLOCKS, LANES), 1)
    even = lane % 2 == 0
    first = jnp.zeros((BLOCKS, LANES), jnp.float32)
    second = jnp.zeros((BLOCKS, LANES), jnp.float32)
    for j in range(MODES):
        scale = 1.0 / jnp.sqrt(energies[j])
        amp_real = vec_real[j] * scale
        amp_imag = vec_imag[j] * scale
        on_real = jnp.where(even, amp_real, amp_imag)
        on_imag = jnp.where(even, -amp_imag, amp_real)
        if j:
            on_real = pltpu.roll(on_real, ROWS * j, 1)
            on_imag = pltpu.roll(on_imag, ROWS * j, 1)
        here = lane // ROWS == j
        first = jnp.where(here, on_real, first)
        second = jnp.where(here, on_imag, second)
    shape = (BLOCKS, ROWS, LANES)
    row = lax.broadcasted_iota(jnp.int32, shape, 1)
    column = lax.broadcasted_iota(jnp.int32, shape, 2)
    whole = jnp.where(
        row % 2 == 0,
        jnp.broadcast_to(first[:, None, :], shape),
        jnp.broadcast_to(second[:, None, :], shape),
    )
    whole = jnp.where(row // 2 == column % ROWS // 2, whole, 0.0)
    turned = whole.reshape(BLOCKS * ROWS, LANES).T
    for j in range(MODES):
        for half in range(2):
            piece = turned[ROWS * j : ROWS * (j + 1), half * LANES : (half + 1) * LANES]
            order_ref[half, pl.ds(j, ROWS, stride=MODES), :] = piece
    return jnp.concatenate([order_ref[0], order_ref[1]], axis=1).astype(jnp.bfloat16)


def spectra_kernel(
    cut,
    scale,
    table_ref,
    series_ref,
    mine_ref,
    coef_ref,
    energy_ref,
    taken_ref,
    made_ref,
    total_ref,
    packed_ref,
    gram_ref,
    order_ref,
    take_sem,
    send_sem,
    recv_sem,
    sum_send_sem,
    sum_recv_sem,
):
    chunks = COMPS * CUTS
    here = lax.axis_index("space")
    me = lax.axis_index("tblock")
    level = me // 2
    core = lax.rem(me, 2)

    def peer(dz, dc):
        return lax.rem(level + dz, 8) * 2 + lax.rem(core + dc, 2)

    peers = [(dz, dc) for dz in (4, 3, 5, 2, 6, 1, 7, 0) for dc in (0, 1)][:-2] + [(0, 1)]

    barrier = pltpu.get_barrier_semaphore()
    for dz, dc in peers:
        pl.semaphore_signal(barrier, inc=1, device_id={"tblock": peer(dz, dc)}, device_id_type=MESH)
    for d in range(1, 16):
        pl.semaphore_signal(
            barrier, inc=1, device_id={"space": lax.rem(here + d, 16)}, device_id_type=MESH
        )

    def take(k):
        comp = k // CUTS
        start = pl.multiple_of(lax.rem(k, CUTS) * cut, LANES)
        slot = lax.rem(k, 2)
        return pltpu.make_async_copy(
            series_ref.at[comp, :, pl.ds(start, cut)], taken_ref.at[slot], take_sem.at[slot]
        )

    def send(k, dz, dc):
        to = peer(dz, dc)
        return pltpu.make_async_remote_copy(
            src_ref=made_ref.at[k, to],
            dst_ref=mine_ref.at[k, me],
            send_sem=send_sem.at[k, to],
            recv_sem=recv_sem.at[k, me],
            device_id={"tblock": to},
            device_id_type=MESH,
        )

    def arrival(k, dz, dc):
        sender = peer(dz, dc)
        return pltpu.make_async_remote_copy(
            src_ref=made_ref.at[k, sender],
            dst_ref=mine_ref.at[k, sender],
            send_sem=send_sem.at[k, sender],
            recv_sem=recv_sem.at[k, sender],
            device_id={"tblock": sender},
            device_id_type=MESH,
        )

    def make(k):
        take(k).wait()
        table = table_ref[...].astype(jnp.bfloat16)
        spectra = jnp.dot(table, taken_ref[lax.rem(k, 2)], preferred_element_type=jnp.float32)
        made_ref[k] = spectra.astype(jnp.bfloat16).reshape(BLOCKS, ROWS, cut)
        mine_ref[k, me] = made_ref[k, me]

    take(0).start()
    take(1).start()
    make(0)
    pl.semaphore_wait(barrier, 30)
    for dz, dc in peers:
        send(0, dz, dc).start()

    def make_and_send(k, carry):
        @pl.when(k + 1 < chunks)
        def _():
            take(k + 1).start()

        make(k)
        for dz, dc in peers:
            send(k, dz, dc).start()
        return carry

    lax.fori_loop(1, chunks, make_and_send, 0)

    total_ref[...] = jnp.zeros_like(total_ref)

    def gather(k, carry):
        for dz, dc in peers:
            arrival(k, dz, dc).wait_recv()
        rows = mine_ref[k].reshape(BLOCKS * ROWS, cut)
        total_ref[...] += lax.dot_general(
            rows, rows, (((1,), (1,)), ((), ())), preferred_element_type=jnp.float32
        )
        return carry

    lax.fori_loop(0, chunks, gather, 0)

    packed_ref[here] = pack_gram(total_ref[...])

    def exchange(d, arriving):
        other = lax.rem(here + d, 16)
        slot = other if arriving else here
        return pltpu.make_async_remote_copy(
            src_ref=packed_ref.at[here],
            dst_ref=packed_ref.at[slot],
            send_sem=sum_send_sem.at[other],
            recv_sem=sum_recv_sem.at[slot],
            device_id={"space": other},
            device_id_type=MESH,
        )

    for d in range(1, 16):
        exchange(d, False).start()
    for d in range(1, 16):
        exchange(d, True).wait_recv()
    packed = packed_ref[0]
    for s in range(1, 16):
        packed = packed + packed_ref[s]
    packed = packed / scale

    vec_real, vec_imag, energies = leading_modes(packed, gram_ref)
    coef_ref[...] = coefficient_matrix(vec_real, vec_imag, energies, order_ref)
    wide = jnp.concatenate(energies, axis=0)
    lane = lax.broadcasted_iota(jnp.int32, (MODES, LANES), 1)
    narrow = wide
    for f in range(1, BINS):
        narrow = jnp.where(lane == f, pltpu.roll(wide, LANES - f, 1), narrow)
    energy_ref[...] = narrow[:, :BINS]

    def finish(k, carry):
        for dz, dc in peers:
            send(k, dz, dc).wait_send()
        return carry

    lax.fori_loop(0, chunks, finish, 0)
    for d in range(1, 16):
        exchange(d, False).wait_send()


def modes_kernel(coef_ref, mine_ref, energy_ref, out_ref, energy_out_ref):
    k = pl.program_id(0)

    @pl.when(k == 0)
    def _():
        energy_out_ref[...] = energy_ref[...]

    rows = mine_ref[k].reshape(BLOCKS * ROWS, mine_ref.shape[3])
    modes = jnp.dot(coef_ref[...], rows, preferred_element_type=jnp.float32)
    modes = modes.astype(jnp.bfloat16)
    for f in range(BINS):
        for part in range(2):
            start = (f * 2 + part) * MODES
            out_ref[f, part, 0] = modes[start : start + MODES]


def local(snapshots, space_count):
    points = snapshots.shape[3]
    cut = points // CUTS
    chunks = COMPS * CUTS
    series = jnp.transpose(snapshots, (0, 2, 1, 3)).reshape(COMPS, STEPS, points)
    vmem = pl.BlockSpec(memory_space=pltpu.VMEM)
    mine, coef, energies = pl.pallas_call(
        functools.partial(spectra_kernel, cut, float(COMPS * points * space_count)),
        out_shape=(
            pltpu.VMEM((chunks, BLOCKS, ROWS, cut), jnp.bfloat16),
            jax.ShapeDtypeStruct((BINS * 2 * MODES, BLOCKS * ROWS), jnp.bfloat16),
            jax.ShapeDtypeStruct((MODES, BINS), jnp.float32),
        ),
        in_specs=[vmem, pl.BlockSpec(memory_space=pltpu.HBM)],
        out_specs=(vmem, vmem, vmem),
        scratch_shapes=[
            pltpu.VMEM((2, STEPS, cut), jnp.bfloat16),
            pltpu.VMEM((chunks, BLOCKS, ROWS, cut), jnp.bfloat16),
            pltpu.VMEM((BLOCKS * ROWS, BLOCKS * ROWS), jnp.float32),
            pltpu.VMEM((16, BLOCKS, BLOCKS * ROWS), jnp.float32),
            pltpu.VMEM((2, BLOCKS, BLOCKS, LANES), jnp.float32),
            pltpu.VMEM((2, BINS * 2 * MODES, LANES), jnp.float32),
            pltpu.SemaphoreType.DMA((2,)),
            pltpu.SemaphoreType.DMA((chunks, 16)),
            pltpu.SemaphoreType.DMA((chunks, 16)),
            pltpu.SemaphoreType.DMA((16,)),
            pltpu.SemaphoreType.DMA((16,)),
        ],
        compiler_params=pltpu.CompilerParams(
            collective_id=0, has_side_effects=True, vmem_limit_bytes=VMEM_BYTES
        ),
        cost_estimate=pl.CostEstimate(
            flops=4 * STEPS * STEPS * COMPS * points,
            bytes_accessed=2 * STEPS * COMPS * points,
            transcendentals=0,
        ),
        name="spectra_exchange",
    )(spectral_table(), series)
    modes, energies = pl.pallas_call(
        modes_kernel,
        grid=(chunks,),
        out_shape=(
            jax.ShapeDtypeStruct((BINS, 2, COMPS, MODES, points), jnp.bfloat16),
            jax.ShapeDtypeStruct((MODES, BINS), jnp.float32),
        ),
        in_specs=[vmem, vmem, vmem],
        out_specs=(
            pl.BlockSpec(
                (BINS, 2, 1, MODES, cut), lambda k: (0, 0, k // CUTS, 0, lax.rem(k, CUTS))
            ),
            vmem,
        ),
        compiler_params=pltpu.CompilerParams(vmem_limit_bytes=VMEM_BYTES),
        cost_estimate=pl.CostEstimate(
            flops=4 * STEPS * BINS * 2 * MODES * COMPS * points,
            bytes_accessed=2 * STEPS * COMPS * points,
            transcendentals=0,
        ),
        name="modes_product",
    )(coef, mine, energies)
    return jnp.transpose(modes, (0, 1, 3, 2, 4)), energies.T


def solution(mesh):
    in_specs = (P("tblock", None, None, "space"),)
    out_specs = (P("tblock", None, None, None, "space"), P("tblock", None))
    body = functools.partial(local, space_count=mesh.shape["space"])
    return jax.shard_map(body, mesh=mesh, in_specs=in_specs, out_specs=out_specs, check_vma=False)
```

```python
import functools
import math

import jax
import jax.numpy as jnp
import numpy as np
from jax import lax
from jax.experimental import pallas as pl
from jax.experimental.pallas import tpu as pltpu
from jax.sharding import PartitionSpec as P

MODES = 4
SUBSPACE_ITERS = 6
BLOCKS = 16
STEPS = 256
BINS = 8
ROWS = 2 * BINS
COMPS = 3
CUTS = 2
LANES = 128
MESH = pl.DeviceIdType.MESH
VMEM_BYTES = 44 * 2**20


def spectral_table():
    times = np.arange(STEPS, dtype=np.int32)
    orders = np.arange(1, STEPS // 2 + 1, dtype=np.int32)
    phase = orders[:, None] * times[None, :] % STEPS
    angle = np.float32(2.0 * math.pi / STEPS) * phase.astype(np.float32)
    swing = np.cos(np.float32(2.0 * math.pi / STEPS) * times.astype(np.float32))
    window = np.float32(0.5) - np.float32(0.5) * swing
    scaled = window / np.float32(math.sqrt(0.375 * STEPS))
    rows = np.stack([scaled * np.cos(angle), -scaled * np.sin(angle)], axis=1)
    return jnp.asarray(rows.reshape(STEPS, STEPS).astype(np.float32))


def pack_gram(total):
    width = total.shape[1]
    cube = total.reshape(BLOCKS, ROWS, width)
    row = lax.broadcasted_iota(jnp.int32, (ROWS, width), 0)
    lane = lax.broadcasted_iota(jnp.int32, (ROWS, width), 1) % ROWS
    same_bin = row // 2 == lane // 2
    same_part = row % 2 == lane % 2
    first = jnp.where(same_bin & same_part, 1.0, 0.0)
    other = jnp.where(same_bin & (row % 2 < lane % 2), 1.0, 0.0)
    other = jnp.where(same_bin & (row % 2 > lane % 2), -1.0, other)
    real = jnp.sum(cube * first[None], axis=1)
    imag = jnp.sum(cube * other[None], axis=1)
    even = lax.broadcasted_iota(jnp.int32, (BLOCKS, width), 1) % 2 == 0
    real = real + pltpu.roll(real, width - 1, 1)
    imag = imag + pltpu.roll(imag, 1, 1)
    return jnp.where(even, real, imag)


def column_sum(value):
    return jnp.sum(value, axis=0, keepdims=True)


def leading_modes(packed, gram_ref):
    even = lax.broadcasted_iota(jnp.int32, (BLOCKS, LANES), 1) % 2 == 0
    per_half = LANES // ROWS
    for half in range(2):
        part = packed[:, half * LANES : (half + 1) * LANES]
        real = jnp.where(even, part, pltpu.roll(part, 1, 1))
        imag = jnp.where(even, pltpu.roll(part, LANES - 1, 1), part)
        for near in range(per_half):
            shift = (LANES - ROWS * near) % LANES
            block = half * per_half + near
            gram_ref[0, block] = real if shift == 0 else pltpu.roll(real, shift, 1)
            gram_ref[1, block] = imag if shift == 0 else pltpu.roll(imag, shift, 1)

    def apply_gram(vec_real, vec_imag):
        out_real = [None] * MODES
        out_imag = [None] * MODES
        for block in range(BLOCKS):
            real = gram_ref[0, block]
            imag = gram_ref[1, block]
            for j in range(MODES):
                row_real = vec_real[j][block : block + 1]
                row_imag = vec_imag[j][block : block + 1]
                term_real = real * row_real - imag * row_imag
                term_imag = real * row_imag + imag * row_real
                out_real[j] = term_real if block == 0 else out_real[j] + term_real
                out_imag[j] = term_imag if block == 0 else out_imag[j] + term_imag
        return out_real, out_imag

    def orthonormal(vec_real, vec_imag):
        vec_real = list(vec_real)
        vec_imag = list(vec_imag)
        for i in range(MODES):
            base_real = vec_real[i]
            base_imag = vec_imag[i]
            square = column_sum(base_real * base_real + base_imag * base_imag)
            inverse = 1.0 / square
            for j in range(i + 1, MODES):
                proj_real = column_sum(base_real * vec_real[j] + base_imag * vec_imag[j]) * inverse
                proj_imag = column_sum(base_real * vec_imag[j] - base_imag * vec_real[j]) * inverse
                vec_real[j] = vec_real[j] - (base_real * proj_real - base_imag * proj_imag)
                vec_imag[j] = vec_imag[j] - (base_real * proj_imag + base_imag * proj_real)
            scale = lax.rsqrt(square)
            vec_real[i] = base_real * scale
            vec_imag[i] = base_imag * scale
        return vec_real, vec_imag

    wide_real = [gram_ref[0, j] for j in range(MODES)]
    wide_imag = [gram_ref[1, j] for j in range(MODES)]
    vec_real, vec_imag = orthonormal(wide_real, wide_imag)

    def sweep(_, carry):
        return orthonormal(*apply_gram(*carry))

    vec_real, vec_imag = lax.fori_loop(1, SUBSPACE_ITERS, sweep, (vec_real, vec_imag))
    wide_real, wide_imag = apply_gram(vec_real, vec_imag)
    energies = [
        column_sum(vec_real[j] * wide_real[j] + vec_imag[j] * wide_imag[j]) for j in range(MODES)
    ]
    return vec_real, vec_imag, energies


def coefficient_matrix(vec_real, vec_imag, energies, order_ref):
    lane = lax.broadcasted_iota(jnp.int32, (BLOCKS, LANES), 1)
    even = lane % 2 == 0
    first = jnp.zeros((BLOCKS, LANES), jnp.float32)
    second = jnp.zeros((BLOCKS, LANES), jnp.float32)
    for j in range(MODES):
        scale = 1.0 / jnp.sqrt(energies[j])
        amp_real = vec_real[j] * scale
        amp_imag = vec_imag[j] * scale
        on_real = jnp.where(even, amp_real, amp_imag)
        on_imag = jnp.where(even, -amp_imag, amp_real)
        if j:
            on_real = pltpu.roll(on_real, ROWS * j, 1)
            on_imag = pltpu.roll(on_imag, ROWS * j, 1)
        here = lane // ROWS == j
        first = jnp.where(here, on_real, first)
        second = jnp.where(here, on_imag, second)
    shape = (BLOCKS, ROWS, LANES)
    row = lax.broadcasted_iota(jnp.int32, shape, 1)
    column = lax.broadcasted_iota(jnp.int32, shape, 2)
    whole = jnp.where(
        row % 2 == 0,
        jnp.broadcast_to(first[:, None, :], shape),
        jnp.broadcast_to(second[:, None, :], shape),
    )
    whole = jnp.where(row // 2 == column % ROWS // 2, whole, 0.0)
    turned = whole.reshape(BLOCKS * ROWS, LANES).T
    for j in range(MODES):
        for half in range(2):
            piece = turned[ROWS * j : ROWS * (j + 1), half * LANES : (half + 1) * LANES]
            order_ref[half, pl.ds(j, ROWS, stride=MODES), :] = piece
    return jnp.concatenate([order_ref[0], order_ref[1]], axis=1).astype(jnp.bfloat16)


def spectra_kernel(
    cut,
    scale,
    table_ref,
    series_ref,
    mine_ref,
    coef_ref,
    energy_ref,
    taken_ref,
    made_ref,
    total_ref,
    packed_ref,
    gram_ref,
    order_ref,
    take_sem,
    send_sem,
    recv_sem,
    sum_send_sem,
    sum_recv_sem,
):
    chunks = COMPS * CUTS
    here = lax.axis_index("space")
    me = lax.axis_index("tblock")
    level = me // 2
    core = lax.rem(me, 2)

    def peer(dz, dc):
        return lax.rem(level + dz, 8) * 2 + lax.rem(core + dc, 2)

    peers = [(dz, dc) for dz in (4, 3, 5, 2, 6, 1, 7, 0) for dc in (0, 1)][:-2] + [(0, 1)]

    def take(k):
        comp = k // CUTS
        start = pl.multiple_of(lax.rem(k, CUTS) * cut, LANES)
        slot = lax.rem(k, 2)
        return pltpu.make_async_copy(
            series_ref.at[comp, :, pl.ds(start, cut)], taken_ref.at[slot], take_sem.at[slot]
        )

    def send(k, dz, dc):
        to = peer(dz, dc)
        return pltpu.make_async_remote_copy(
            src_ref=made_ref.at[k, to],
            dst_ref=mine_ref.at[k, me],
            send_sem=send_sem.at[k, to],
            recv_sem=recv_sem.at[k, me],
            device_id={"tblock": to},
            device_id_type=MESH,
        )

    def arrival(k, dz, dc):
        sender = peer(dz, dc)
        return pltpu.make_async_remote_copy(
            src_ref=made_ref.at[k, sender],
            dst_ref=mine_ref.at[k, sender],
            send_sem=send_sem.at[k, sender],
            recv_sem=recv_sem.at[k, sender],
            device_id={"tblock": sender},
            device_id_type=MESH,
        )

    def make(k):
        take(k).wait()
        table = table_ref[...].astype(jnp.bfloat16)
        spectra = jnp.dot(table, taken_ref[lax.rem(k, 2)], preferred_element_type=jnp.float32)
        made_ref[k] = spectra.astype(jnp.bfloat16).reshape(BLOCKS, ROWS, cut)
        mine_ref[k, me] = made_ref[k, me]

    take(0).start()
    take(1).start()
    barrier = pltpu.get_barrier_semaphore()
    for dz, dc in peers:
        pl.semaphore_signal(barrier, inc=1, device_id={"tblock": peer(dz, dc)}, device_id_type=MESH)
    for d in range(1, 16):
        pl.semaphore_signal(
            barrier, inc=1, device_id={"space": lax.rem(here + d, 16)}, device_id_type=MESH
        )

    make(0)
    pl.semaphore_wait(barrier, 30)
    for dz, dc in peers:
        send(0, dz, dc).start()

    def make_and_send(k, carry):
        @pl.when(k + 1 < chunks)
        def _():
            take(k + 1).start()

        make(k)
        for dz, dc in peers:
            send(k, dz, dc).start()
        return carry

    lax.fori_loop(1, chunks, make_and_send, 0)

    total_ref[...] = jnp.zeros_like(total_ref)

    def gather(k, carry):
        for dz, dc in peers:
            arrival(k, dz, dc).wait_recv()
        rows = mine_ref[k].reshape(BLOCKS * ROWS, cut)
        total_ref[...] += lax.dot_general(
            rows, rows, (((1,), (1,)), ((), ())), preferred_element_type=jnp.float32
        )
        return carry

    lax.fori_loop(0, chunks, gather, 0)

    packed_ref[here] = pack_gram(total_ref[...])

    def exchange(d, arriving):
        other = lax.rem(here + d, 16)
        slot = other if arriving else here
        return pltpu.make_async_remote_copy(
            src_ref=packed_ref.at[here],
            dst_ref=packed_ref.at[slot],
            send_sem=sum_send_sem.at[other],
            recv_sem=sum_recv_sem.at[slot],
            device_id={"space": other},
            device_id_type=MESH,
        )

    for d in range(1, 16):
        exchange(d, False).start()
    for d in range(1, 16):
        exchange(d, True).wait_recv()
    packed = packed_ref[0]
    for s in range(1, 16):
        packed = packed + packed_ref[s]
    packed = packed / scale

    vec_real, vec_imag, energies = leading_modes(packed, gram_ref)
    coef_ref[...] = coefficient_matrix(vec_real, vec_imag, energies, order_ref)
    wide = jnp.concatenate(energies, axis=0)
    lane = lax.broadcasted_iota(jnp.int32, (MODES, LANES), 1)
    narrow = wide
    for f in range(1, BINS):
        narrow = jnp.where(lane == f, pltpu.roll(wide, LANES - f, 1), narrow)
    energy_ref[...] = narrow[:, :BINS]

    def finish(k, carry):
        for dz, dc in peers:
            send(k, dz, dc).wait_send()
        return carry

    lax.fori_loop(0, chunks, finish, 0)
    for d in range(1, 16):
        exchange(d, False).wait_send()


def modes_kernel(coef_ref, mine_ref, energy_ref, out_ref, energy_out_ref, held_ref, sem):
    chunks, cut = mine_ref.shape[0], mine_ref.shape[3]

    def put(k):
        columns = pl.ds(k % CUTS * cut, cut)
        return pltpu.make_async_copy(
            held_ref.at[k], out_ref.at[:, :, k // CUTS, :, columns], sem.at[k]
        )

    for k in range(chunks):
        rows = mine_ref[k].reshape(BLOCKS * ROWS, cut)
        modes = jnp.dot(coef_ref[...], rows, preferred_element_type=jnp.float32)
        modes = modes.astype(jnp.bfloat16)
        for f in range(BINS):
            for part in range(2):
                start = (f * 2 + part) * MODES
                held_ref[k, f, part] = modes[start : start + MODES]
        put(k).start()
    energy_out_ref[...] = energy_ref[...]
    for k in range(chunks):
        put(k).wait()


def local(snapshots, space_count):
    points = snapshots.shape[3]
    cut = points // CUTS
    chunks = COMPS * CUTS
    series = jnp.transpose(snapshots, (0, 2, 1, 3)).reshape(COMPS, STEPS, points)
    vmem = pl.BlockSpec(memory_space=pltpu.VMEM)
    mine, coef, energies = pl.pallas_call(
        functools.partial(spectra_kernel, cut, float(COMPS * points * space_count)),
        out_shape=(
            pltpu.VMEM((chunks, BLOCKS, ROWS, cut), jnp.bfloat16),
            jax.ShapeDtypeStruct((BINS * 2 * MODES, BLOCKS * ROWS), jnp.bfloat16),
            jax.ShapeDtypeStruct((MODES, BINS), jnp.float32),
        ),
        in_specs=[vmem, pl.BlockSpec(memory_space=pltpu.HBM)],
        out_specs=(vmem, vmem, vmem),
        scratch_shapes=[
            pltpu.VMEM((2, STEPS, cut), jnp.bfloat16),
            pltpu.VMEM((chunks, BLOCKS, ROWS, cut), jnp.bfloat16),
            pltpu.VMEM((BLOCKS * ROWS, BLOCKS * ROWS), jnp.float32),
            pltpu.VMEM((16, BLOCKS, BLOCKS * ROWS), jnp.float32),
            pltpu.VMEM((2, BLOCKS, BLOCKS, LANES), jnp.float32),
            pltpu.VMEM((2, BINS * 2 * MODES, LANES), jnp.float32),
            pltpu.SemaphoreType.DMA((2,)),
            pltpu.SemaphoreType.DMA((chunks, 16)),
            pltpu.SemaphoreType.DMA((chunks, 16)),
            pltpu.SemaphoreType.DMA((16,)),
            pltpu.SemaphoreType.DMA((16,)),
        ],
        compiler_params=pltpu.CompilerParams(
            collective_id=0, has_side_effects=True, vmem_limit_bytes=VMEM_BYTES
        ),
        cost_estimate=pl.CostEstimate(
            flops=4 * STEPS * STEPS * COMPS * points,
            bytes_accessed=2 * STEPS * COMPS * points,
            transcendentals=0,
        ),
        name="spectra_exchange",
    )(spectral_table(), series)
    modes, energies = pl.pallas_call(
        modes_kernel,
        out_shape=(
            jax.ShapeDtypeStruct((BINS, 2, COMPS, MODES, points), jnp.bfloat16),
            jax.ShapeDtypeStruct((MODES, BINS), jnp.float32),
        ),
        in_specs=[vmem, vmem, vmem],
        out_specs=(pl.BlockSpec(memory_space=pltpu.HBM), vmem),
        scratch_shapes=[
            pltpu.VMEM((chunks, BINS, 2, MODES, cut), jnp.bfloat16),
            pltpu.SemaphoreType.DMA((chunks,)),
        ],
        compiler_params=pltpu.CompilerParams(vmem_limit_bytes=VMEM_BYTES),
        cost_estimate=pl.CostEstimate(
            flops=4 * STEPS * BINS * 2 * MODES * COMPS * points,
            bytes_accessed=2 * STEPS * COMPS * points,
            transcendentals=0,
        ),
        name="modes_product",
    )(coef, mine, energies)
    return jnp.transpose(modes, (0, 1, 3, 2, 4)), energies.T


def solution(mesh):
    in_specs = (P("tblock", None, None, "space"),)
    out_specs = (P("tblock", None, None, None, "space"), P("tblock", None))
    body = functools.partial(local, space_count=mesh.shape["space"])
    return jax.shard_map(body, mesh=mesh, in_specs=in_specs, out_specs=out_specs, check_vma=False)
```

```python
import functools
import math

import jax
import jax.numpy as jnp
import numpy as np
from jax import lax
from jax.experimental import pallas as pl
from jax.experimental.pallas import tpu as pltpu
from jax.sharding import PartitionSpec as P

MODES = 4
SUBSPACE_ITERS = 6
BLOCKS = 16
STEPS = 256
BINS = 8
ROWS = 2 * BINS
COMPS = 3
CUTS = 2
LEVELS = 8
SIDE = 4
LANES = 128
MESH = pl.DeviceIdType.MESH
VMEM_BYTES = 44 * 2**20


def spectral_table():
    times = np.arange(STEPS, dtype=np.int32)
    orders = np.arange(1, STEPS // 2 + 1, dtype=np.int32)
    phase = orders[:, None] * times[None, :] % STEPS
    angle = np.float32(2.0 * math.pi / STEPS) * phase.astype(np.float32)
    swing = np.cos(np.float32(2.0 * math.pi / STEPS) * times.astype(np.float32))
    window = np.float32(0.5) - np.float32(0.5) * swing
    scaled = window / np.float32(math.sqrt(0.375 * STEPS))
    rows = np.stack([scaled * np.cos(angle), -scaled * np.sin(angle)], axis=1)
    return jnp.asarray(rows.reshape(STEPS, STEPS).astype(np.float32))


def chunk_widths(points):
    first, last = 4 * LANES, 8 * LANES
    return ((first, points - first), (points,), (points - last, last))


def pack_gram(total):
    width = total.shape[1]
    cube = total.reshape(BLOCKS, ROWS, width)
    row = lax.broadcasted_iota(jnp.int32, (ROWS, width), 0)
    lane = lax.broadcasted_iota(jnp.int32, (ROWS, width), 1) % ROWS
    same_bin = row // 2 == lane // 2
    same_part = row % 2 == lane % 2
    first = jnp.where(same_bin & same_part, 1.0, 0.0)
    other = jnp.where(same_bin & (row % 2 < lane % 2), 1.0, 0.0)
    other = jnp.where(same_bin & (row % 2 > lane % 2), -1.0, other)
    real = jnp.sum(cube * first[None], axis=1)
    imag = jnp.sum(cube * other[None], axis=1)
    even = lax.broadcasted_iota(jnp.int32, (BLOCKS, width), 1) % 2 == 0
    real = real + pltpu.roll(real, width - 1, 1)
    imag = imag + pltpu.roll(imag, 1, 1)
    return jnp.where(even, real, imag)


def column_sum(value):
    return jnp.sum(value, axis=0, keepdims=True)


def leading_modes(packed, gram_ref):
    even = lax.broadcasted_iota(jnp.int32, (BLOCKS, LANES), 1) % 2 == 0
    per_half = LANES // ROWS
    for half in range(2):
        part = packed[:, half * LANES : (half + 1) * LANES]
        real = jnp.where(even, part, pltpu.roll(part, 1, 1))
        imag = jnp.where(even, pltpu.roll(part, LANES - 1, 1), part)
        for near in range(per_half):
            shift = (LANES - ROWS * near) % LANES
            block = half * per_half + near
            gram_ref[0, block] = real if shift == 0 else pltpu.roll(real, shift, 1)
            gram_ref[1, block] = imag if shift == 0 else pltpu.roll(imag, shift, 1)

    def apply_gram(vec_real, vec_imag):
        out_real = [None] * MODES
        out_imag = [None] * MODES
        for block in range(BLOCKS):
            real = gram_ref[0, block]
            imag = gram_ref[1, block]
            for j in range(MODES):
                row_real = vec_real[j][block : block + 1]
                row_imag = vec_imag[j][block : block + 1]
                term_real = real * row_real - imag * row_imag
                term_imag = real * row_imag + imag * row_real
                out_real[j] = term_real if block == 0 else out_real[j] + term_real
                out_imag[j] = term_imag if block == 0 else out_imag[j] + term_imag
        return out_real, out_imag

    def orthonormal(vec_real, vec_imag):
        vec_real = list(vec_real)
        vec_imag = list(vec_imag)
        for i in range(MODES):
            base_real = vec_real[i]
            base_imag = vec_imag[i]
            square = column_sum(base_real * base_real + base_imag * base_imag)
            inverse = 1.0 / square
            for j in range(i + 1, MODES):
                proj_real = column_sum(base_real * vec_real[j] + base_imag * vec_imag[j]) * inverse
                proj_imag = column_sum(base_real * vec_imag[j] - base_imag * vec_real[j]) * inverse
                vec_real[j] = vec_real[j] - (base_real * proj_real - base_imag * proj_imag)
                vec_imag[j] = vec_imag[j] - (base_real * proj_imag + base_imag * proj_real)
            scale = lax.rsqrt(square)
            vec_real[i] = base_real * scale
            vec_imag[i] = base_imag * scale
        return vec_real, vec_imag

    wide_real = [gram_ref[0, j] for j in range(MODES)]
    wide_imag = [gram_ref[1, j] for j in range(MODES)]
    vec_real, vec_imag = orthonormal(wide_real, wide_imag)

    def sweep(_, carry):
        return orthonormal(*apply_gram(*carry))

    vec_real, vec_imag = lax.fori_loop(1, SUBSPACE_ITERS, sweep, (vec_real, vec_imag))
    wide_real, wide_imag = apply_gram(vec_real, vec_imag)
    energies = [
        column_sum(vec_real[j] * wide_real[j] + vec_imag[j] * wide_imag[j]) for j in range(MODES)
    ]
    return vec_real, vec_imag, energies


def coefficient_matrix(vec_real, vec_imag, energies, order_ref):
    lane = lax.broadcasted_iota(jnp.int32, (BLOCKS, LANES), 1)
    even = lane % 2 == 0
    first = jnp.zeros((BLOCKS, LANES), jnp.float32)
    second = jnp.zeros((BLOCKS, LANES), jnp.float32)
    for j in range(MODES):
        scale = 1.0 / jnp.sqrt(energies[j])
        amp_real = vec_real[j] * scale
        amp_imag = vec_imag[j] * scale
        on_real = jnp.where(even, amp_real, amp_imag)
        on_imag = jnp.where(even, -amp_imag, amp_real)
        if j:
            on_real = pltpu.roll(on_real, ROWS * j, 1)
            on_imag = pltpu.roll(on_imag, ROWS * j, 1)
        here = lane // ROWS == j
        first = jnp.where(here, on_real, first)
        second = jnp.where(here, on_imag, second)
    shape = (BLOCKS, ROWS, LANES)
    row = lax.broadcasted_iota(jnp.int32, shape, 1)
    column = lax.broadcasted_iota(jnp.int32, shape, 2)
    whole = jnp.where(
        row % 2 == 0,
        jnp.broadcast_to(first[:, None, :], shape),
        jnp.broadcast_to(second[:, None, :], shape),
    )
    whole = jnp.where(row // 2 == column % ROWS // 2, whole, 0.0)
    turned = whole.reshape(BLOCKS * ROWS, LANES).T
    for j in range(MODES):
        for half in range(2):
            piece = turned[ROWS * j : ROWS * (j + 1), half * LANES : (half + 1) * LANES]
            order_ref[half, pl.ds(j, ROWS, stride=MODES), :] = piece
    return jnp.concatenate([order_ref[0], order_ref[1]], axis=1).astype(jnp.bfloat16)


def spectra_kernel(
    points,
    scale,
    table_ref,
    series_ref,
    mine_ref,
    coef_ref,
    energy_ref,
    rows_ref,
    round_ref,
    taken_ref,
    made_ref,
    total_ref,
    packed_ref,
    gram_ref,
    order_ref,
    table_sem,
    take_sem,
    send_sem,
    recv_sem,
    sum_send_sem,
    sum_recv_sem,
    ring_sem,
    plane_sem,
):
    chunks = []
    for comp, widths in enumerate(chunk_widths(points)):
        start = 0
        for width in widths:
            chunks.append((comp, start, width))
            start += width
    here = lax.axis_index("space")
    me = lax.axis_index("tblock")
    level = me // 2
    core = lax.rem(me, 2)
    high = here // SIDE
    wide = lax.rem(here, SIDE)

    def peer(dz, dc):
        return lax.rem(level + dz, LEVELS) * 2 + lax.rem(core + dc, 2)

    def plane(dy, dx):
        return lax.rem(high + dy, SIDE) * SIDE + lax.rem(wide + dx, SIDE)

    def signal(sem, **device):
        pl.semaphore_signal(sem, inc=1, device_id=device, device_id_type=MESH)

    rings = [[(0, 1)]] + [
        [(dz, dc) for dz in sorted({far, LEVELS - far}) for dc in (0, 1)]
        for far in range(1, LEVELS // 2 + 1)
    ]
    rings = [rings[1] + rings[0]] + rings[2:]
    peers = [pair for ring in rings[::-1] for pair in ring]

    def take(k):
        comp, start, width = chunks[k]
        return pltpu.make_async_copy(
            series_ref.at[comp, :, pl.ds(start, width)],
            taken_ref.at[k % 2, :, pl.ds(0, width)],
            take_sem.at[k % 2],
        )

    def columns(k):
        comp, start, width = chunks[k]
        return pl.ds(comp * points + start, width)

    def send(k, dz, dc):
        to = peer(dz, dc)
        return pltpu.make_async_remote_copy(
            src_ref=made_ref.at[to, :, columns(k)],
            dst_ref=mine_ref.at[me, :, columns(k)],
            send_sem=send_sem.at[k, to],
            recv_sem=recv_sem.at[k, me],
            device_id={"tblock": to},
            device_id_type=MESH,
        )

    def arrival(k, dz, dc):
        sender = peer(dz, dc)
        return pltpu.make_async_remote_copy(
            src_ref=made_ref.at[sender, :, columns(k)],
            dst_ref=mine_ref.at[sender, :, columns(k)],
            send_sem=send_sem.at[k, sender],
            recv_sem=recv_sem.at[k, sender],
            device_id={"tblock": sender},
            device_id_type=MESH,
        )

    def make(k):
        width = chunks[k][2]
        take(k).wait()
        spectra = jnp.dot(
            round_ref[...], taken_ref[k % 2, :, :width], preferred_element_type=jnp.float32
        )
        made_ref[:, :, columns(k)] = spectra.astype(jnp.bfloat16).reshape(BLOCKS, ROWS, width)
        if k + 2 < len(chunks):
            take(k + 2).start()
        mine_ref[me, :, columns(k)] = made_ref[me, :, columns(k)]

    table = pltpu.make_async_copy(table_ref, rows_ref, table_sem)
    table.start()
    take(0).start()
    barrier = pltpu.get_barrier_semaphore()
    for dz, dc in rings[0]:
        signal(barrier, tblock=peer(dz, dc))
    sides = [(0, 1), (0, SIDE - 1), (1, 0), (SIDE - 1, 0)]
    for dy, dx in sides:
        signal(barrier, space=plane(dy, dx))
    take(1).start()
    table.wait()
    round_ref[...] = rows_ref[...].astype(jnp.bfloat16)
    make(0)
    pl.semaphore_wait(barrier, len(rings[0]) + len(sides))

    for r, ring in enumerate(rings):
        if r:
            pl.semaphore_wait(ring_sem.at[r - 1, 0], 1)
            pl.semaphore_wait(ring_sem.at[r - 1, 1], 1)
        if r + 1 < len(rings):
            signal(ring_sem.at[r, 0], tblock=peer(1, 0))
            signal(ring_sem.at[r, 1], tblock=peer(LEVELS - 1, 0))
        for dz, dc in ring:
            send(0, dz, dc).start()
        if r == 0:
            signal(plane_sem.at[0], space=plane(0, SIDE - 1))
    for k in range(1, len(chunks)):
        make(k)
        for dz, dc in peers:
            send(k, dz, dc).start()
        if k == 1:
            pl.semaphore_wait(plane_sem.at[0], 1)
            signal(plane_sem.at[1], space=plane(1, 0))
            signal(plane_sem.at[2], space=plane(SIDE - 1, 0))
        if k == 2:
            pl.semaphore_wait(plane_sem.at[1], 1)
            pl.semaphore_wait(plane_sem.at[2], 1)
            signal(plane_sem.at[3], space=plane(SIDE - 1, 0))
    pl.semaphore_wait(plane_sem.at[3], 1)

    for k in range(len(chunks)):
        for dz, dc in peers:
            arrival(k, dz, dc).wait_recv()
        rows = mine_ref[:, :, columns(k)].reshape(BLOCKS * ROWS, chunks[k][2])
        part = lax.dot_general(
            rows, rows, (((1,), (1,)), ((), ())), preferred_element_type=jnp.float32
        )
        if k == 0:
            total_ref[...] = part
        else:
            total_ref[...] += part

    packed_ref[here] = pack_gram(total_ref[...])

    def exchange(d, arriving):
        other = lax.rem(here + d, SIDE * SIDE)
        slot = other if arriving else here
        return pltpu.make_async_remote_copy(
            src_ref=packed_ref.at[here],
            dst_ref=packed_ref.at[slot],
            send_sem=sum_send_sem.at[other],
            recv_sem=sum_recv_sem.at[slot],
            device_id={"space": other},
            device_id_type=MESH,
        )

    others = range(1, SIDE * SIDE)
    for d in others:
        exchange(d, False).start()
    for d in others:
        exchange(d, True).wait_recv()
    packed = packed_ref[0]
    for s in others:
        packed = packed + packed_ref[s]
    packed = packed / scale

    vec_real, vec_imag, energies = leading_modes(packed, gram_ref)
    coef_ref[...] = coefficient_matrix(vec_real, vec_imag, energies, order_ref)
    spread = jnp.concatenate(energies, axis=0)
    lane = lax.broadcasted_iota(jnp.int32, (MODES, LANES), 1)
    narrow = spread
    for f in range(1, BINS):
        narrow = jnp.where(lane == f, pltpu.roll(spread, LANES - f, 1), narrow)
    energy_ref[...] = narrow[:, :BINS]

    for k in range(len(chunks)):
        for dz, dc in peers:
            send(k, dz, dc).wait_send()
    for d in others:
        exchange(d, False).wait_send()


def modes_kernel(coef_ref, mine_ref, energy_ref, out_ref, energy_out_ref, held_ref, sem):
    chunks, cut = held_ref.shape[0], held_ref.shape[4]

    def put(k):
        columns = pl.ds(k % CUTS * cut, cut)
        return pltpu.make_async_copy(
            held_ref.at[k], out_ref.at[:, :, k // CUTS, :, columns], sem.at[k]
        )

    for k in range(chunks):
        rows = mine_ref[:, :, k * cut : (k + 1) * cut].reshape(BLOCKS * ROWS, cut)
        modes = jnp.dot(coef_ref[...], rows, preferred_element_type=jnp.float32)
        modes = modes.astype(jnp.bfloat16)
        for f in range(BINS):
            for part in range(2):
                start = (f * 2 + part) * MODES
                held_ref[k, f, part] = modes[start : start + MODES]
        put(k).start()
    energy_out_ref[...] = energy_ref[...]
    for k in range(chunks):
        put(k).wait()


def local(snapshots, space_count):
    points = snapshots.shape[3]
    cut = points // CUTS
    width = COMPS * points
    pieces = len([w for widths in chunk_widths(points) for w in widths])
    series = jnp.transpose(snapshots, (0, 2, 1, 3)).reshape(COMPS, STEPS, points)
    vmem = pl.BlockSpec(memory_space=pltpu.VMEM)
    hbm = pl.BlockSpec(memory_space=pltpu.HBM)
    mine, coef, energies = pl.pallas_call(
        functools.partial(spectra_kernel, points, float(width * space_count)),
        out_shape=(
            pltpu.VMEM((BLOCKS, ROWS, width), jnp.bfloat16),
            jax.ShapeDtypeStruct((BINS * 2 * MODES, BLOCKS * ROWS), jnp.bfloat16),
            jax.ShapeDtypeStruct((MODES, BINS), jnp.float32),
        ),
        in_specs=[hbm, hbm],
        out_specs=(vmem, vmem, vmem),
        scratch_shapes=[
            pltpu.VMEM((STEPS, STEPS), jnp.float32),
            pltpu.VMEM((STEPS, STEPS), jnp.bfloat16),
            pltpu.VMEM((2, STEPS, points), jnp.bfloat16),
            pltpu.VMEM((BLOCKS, ROWS, width), jnp.bfloat16),
            pltpu.VMEM((BLOCKS * ROWS, BLOCKS * ROWS), jnp.float32),
            pltpu.VMEM((SIDE * SIDE, BLOCKS, BLOCKS * ROWS), jnp.float32),
            pltpu.VMEM((2, BLOCKS, BLOCKS, LANES), jnp.float32),
            pltpu.VMEM((2, BINS * 2 * MODES, LANES), jnp.float32),
            pltpu.SemaphoreType.DMA,
            pltpu.SemaphoreType.DMA((2,)),
            pltpu.SemaphoreType.DMA((pieces, BLOCKS)),
            pltpu.SemaphoreType.DMA((pieces, BLOCKS)),
            pltpu.SemaphoreType.DMA((SIDE * SIDE,)),
            pltpu.SemaphoreType.DMA((SIDE * SIDE,)),
            pltpu.SemaphoreType.REGULAR((LEVELS // 2 - 1, 2)),
            pltpu.SemaphoreType.REGULAR((4,)),
        ],
        compiler_params=pltpu.CompilerParams(
            collective_id=0, has_side_effects=True, vmem_limit_bytes=VMEM_BYTES
        ),
        cost_estimate=pl.CostEstimate(
            flops=4 * STEPS * STEPS * COMPS * points,
            bytes_accessed=2 * STEPS * COMPS * points,
            transcendentals=0,
        ),
        name="spectra_exchange",
    )(spectral_table(), series)
    modes, energies = pl.pallas_call(
        modes_kernel,
        out_shape=(
            jax.ShapeDtypeStruct((BINS, 2, COMPS, MODES, points), jnp.bfloat16),
            jax.ShapeDtypeStruct((MODES, BINS), jnp.float32),
        ),
        in_specs=[vmem, vmem, vmem],
        out_specs=(hbm, vmem),
        scratch_shapes=[
            pltpu.VMEM((COMPS * CUTS, BINS, 2, MODES, cut), jnp.bfloat16),
            pltpu.SemaphoreType.DMA((COMPS * CUTS,)),
        ],
        compiler_params=pltpu.CompilerParams(vmem_limit_bytes=VMEM_BYTES),
        cost_estimate=pl.CostEstimate(
            flops=4 * STEPS * BINS * 2 * MODES * COMPS * points,
            bytes_accessed=2 * STEPS * COMPS * points,
            transcendentals=0,
        ),
        name="modes_product",
    )(coef, mine, energies)
    return jnp.transpose(modes, (0, 1, 3, 2, 4)), energies.T


def solution(mesh):
    in_specs = (P("tblock", None, None, "space"),)
    out_specs = (P("tblock", None, None, None, "space"), P("tblock", None))
    body = functools.partial(local, space_count=mesh.shape["space"])
    return jax.shard_map(body, mesh=mesh, in_specs=in_specs, out_specs=out_specs, check_vma=False)
```

```python
import functools
import math

import jax
import jax.numpy as jnp
import numpy as np
from jax import lax
from jax.experimental import pallas as pl
from jax.experimental.pallas import tpu as pltpu
from jax.sharding import PartitionSpec as P

MODES = 4
SUBSPACE_ITERS = 6
BLOCKS = 16
STEPS = 256
BINS = 8
ROWS = 2 * BINS
COMPS = 3
GROUPS = 2
GROUP_BINS = BINS // GROUPS
GROUP_ROWS = ROWS // GROUPS
LEVELS = 8
SIDE = 4
LANES = 128
MESH = pl.DeviceIdType.MESH
VMEM_BYTES = 50 * 2**20
MODES_VMEM_BYTES = 16 * 2**20


def spectral_table():
    times = np.arange(STEPS, dtype=np.int32)
    orders = np.arange(1, STEPS // 2 + 1, dtype=np.int32)
    phase = orders[:, None] * times[None, :] % STEPS
    angle = np.float32(2.0 * math.pi / STEPS) * phase.astype(np.float32)
    swing = np.cos(np.float32(2.0 * math.pi / STEPS) * times.astype(np.float32))
    window = np.float32(0.5) - np.float32(0.5) * swing
    scaled = window / np.float32(math.sqrt(0.375 * STEPS))
    rows = np.stack([scaled * np.cos(angle), -scaled * np.sin(angle)], axis=1)
    rows = rows.reshape(BLOCKS, GROUPS, GROUP_ROWS, STEPS).transpose(1, 0, 2, 3)
    return jnp.asarray(rows.reshape(STEPS, STEPS).astype(np.float32))


def chunk_plan(points):
    half = points // GROUPS
    first, second, last = 2 * LANES, 8 * LANES, 8 * LANES
    made = [(0, 0, first), (0, first, second - first), (0, second, half - second)]
    sent = [(0, start, width) for _, start, width in made] + [(0, half, (COMPS - 1) * half)]
    made += [(c, 0, half) for c in range(1, COMPS)]
    sent += [(1, 0, COMPS * half - last), (1, COMPS * half - last, last)]
    return made, sent


def pack_gram(total):
    width = total.shape[1]
    cube = total.reshape(BLOCKS, ROWS, width)
    row = lax.broadcasted_iota(jnp.int32, (ROWS, width), 0)
    lane = lax.broadcasted_iota(jnp.int32, (ROWS, width), 1) % ROWS
    same_bin = row // 2 == lane // 2
    same_part = row % 2 == lane % 2
    first = jnp.where(same_bin & same_part, 1.0, 0.0)
    other = jnp.where(same_bin & (row % 2 < lane % 2), 1.0, 0.0)
    other = jnp.where(same_bin & (row % 2 > lane % 2), -1.0, other)
    real = jnp.sum(cube * first[None], axis=1)
    imag = jnp.sum(cube * other[None], axis=1)
    even = lax.broadcasted_iota(jnp.int32, (BLOCKS, width), 1) % 2 == 0
    real = real + pltpu.roll(real, width - 1, 1)
    imag = imag + pltpu.roll(imag, 1, 1)
    both = jnp.where(even, real, imag)
    left, right = both[:, :LANES], both[:, LANES:]
    left = left + pltpu.roll(left, LANES - GROUP_ROWS, 1)
    right = right + pltpu.roll(right, GROUP_ROWS, 1)
    return jnp.where(first_half((BLOCKS, LANES)), left, right)


def first_half(shape):
    return lax.broadcasted_iota(jnp.int32, shape, 1) % ROWS < GROUP_ROWS


def column_sum(value):
    return jnp.sum(value, axis=0, keepdims=True)


def leading_modes(packed, gram_ref):
    even = lax.broadcasted_iota(jnp.int32, (BLOCKS, LANES), 1) % 2 == 0
    low = first_half((BLOCKS, LANES))
    per_half = LANES // ROWS
    for half in range(2):
        if half:
            part = jnp.where(low, pltpu.roll(packed, LANES - GROUP_ROWS, 1), packed)
        else:
            part = jnp.where(low, packed, pltpu.roll(packed, GROUP_ROWS, 1))
        real = jnp.where(even, part, pltpu.roll(part, 1, 1))
        imag = jnp.where(even, pltpu.roll(part, LANES - 1, 1), part)
        for near in range(per_half):
            shift = (LANES - ROWS * near) % LANES
            block = half * per_half + near
            gram_ref[0, block] = real if shift == 0 else pltpu.roll(real, shift, 1)
            gram_ref[1, block] = imag if shift == 0 else pltpu.roll(imag, shift, 1)

    def apply_gram(vec_real, vec_imag):
        out_real = [None] * MODES
        out_imag = [None] * MODES
        for block in range(BLOCKS):
            real = gram_ref[0, block]
            imag = gram_ref[1, block]
            for j in range(MODES):
                row_real = vec_real[j][block : block + 1]
                row_imag = vec_imag[j][block : block + 1]
                term_real = real * row_real - imag * row_imag
                term_imag = real * row_imag + imag * row_real
                out_real[j] = term_real if block == 0 else out_real[j] + term_real
                out_imag[j] = term_imag if block == 0 else out_imag[j] + term_imag
        return out_real, out_imag

    def orthonormal(vec_real, vec_imag):
        vec_real = list(vec_real)
        vec_imag = list(vec_imag)
        for i in range(MODES):
            base_real = vec_real[i]
            base_imag = vec_imag[i]
            square = column_sum(base_real * base_real + base_imag * base_imag)
            inverse = 1.0 / square
            for j in range(i + 1, MODES):
                proj_real = column_sum(base_real * vec_real[j] + base_imag * vec_imag[j]) * inverse
                proj_imag = column_sum(base_real * vec_imag[j] - base_imag * vec_real[j]) * inverse
                vec_real[j] = vec_real[j] - (base_real * proj_real - base_imag * proj_imag)
                vec_imag[j] = vec_imag[j] - (base_real * proj_imag + base_imag * proj_real)
            scale = lax.rsqrt(square)
            vec_real[i] = base_real * scale
            vec_imag[i] = base_imag * scale
        return vec_real, vec_imag

    wide_real = [gram_ref[0, j] for j in range(MODES)]
    wide_imag = [gram_ref[1, j] for j in range(MODES)]
    vec_real, vec_imag = orthonormal(wide_real, wide_imag)

    def sweep(_, carry):
        return orthonormal(*apply_gram(*carry))

    vec_real, vec_imag = lax.fori_loop(1, SUBSPACE_ITERS, sweep, (vec_real, vec_imag))
    wide_real, wide_imag = apply_gram(vec_real, vec_imag)
    energies = [
        column_sum(vec_real[j] * wide_real[j] + vec_imag[j] * wide_imag[j]) for j in range(MODES)
    ]
    return vec_real, vec_imag, energies


def coefficient_matrix(vec_real, vec_imag, energies, order_ref):
    lane = lax.broadcasted_iota(jnp.int32, (BLOCKS, LANES), 1)
    even = lane % 2 == 0
    first = jnp.zeros((BLOCKS, LANES), jnp.float32)
    second = jnp.zeros((BLOCKS, LANES), jnp.float32)
    for j in range(MODES):
        scale = 1.0 / jnp.sqrt(energies[j])
        amp_real = vec_real[j] * scale
        amp_imag = vec_imag[j] * scale
        on_real = jnp.where(even, amp_real, amp_imag)
        on_imag = jnp.where(even, -amp_imag, amp_real)
        if j:
            on_real = pltpu.roll(on_real, ROWS * j, 1)
            on_imag = pltpu.roll(on_imag, ROWS * j, 1)
        here = lane // ROWS == j
        first = jnp.where(here, on_real, first)
        second = jnp.where(here, on_imag, second)
    shape = (BLOCKS, ROWS, LANES)
    row = lax.broadcasted_iota(jnp.int32, shape, 1)
    column = lax.broadcasted_iota(jnp.int32, shape, 2)
    whole = jnp.where(
        row % 2 == 0,
        jnp.broadcast_to(first[:, None, :], shape),
        jnp.broadcast_to(second[:, None, :], shape),
    )
    whole = jnp.where(row // 2 == column % ROWS // 2, whole, 0.0)
    turned = whole.reshape(BLOCKS * ROWS, LANES).T
    for j in range(MODES):
        for half in range(2):
            piece = turned[ROWS * j : ROWS * (j + 1), half * LANES : (half + 1) * LANES]
            order_ref[half, pl.ds(j, ROWS, stride=MODES), :] = piece
    return jnp.concatenate([order_ref[0], order_ref[1]], axis=1).astype(jnp.bfloat16)


def group_modes(coef, mine_ref, columns, put):
    rows = mine_ref[:, :, columns]
    rows = rows.reshape(BLOCKS * ROWS, rows.shape[2])
    modes = jnp.dot(coef, rows, preferred_element_type=jnp.float32).astype(jnp.bfloat16)
    for half in range(GROUPS):
        for f in range(GROUP_BINS):
            for part in range(2):
                start = ((half * GROUP_BINS + f) * 2 + part) * MODES
                put(f, part, half, modes[start : start + MODES])


def spectra_kernel(
    points,
    scale,
    table_ref,
    series_ref,
    mine_ref,
    done_ref,
    coef_ref,
    energy_ref,
    rows_ref,
    round_ref,
    taken_ref,
    made_ref,
    early_ref,
    total_ref,
    packed_ref,
    gram_ref,
    order_ref,
    table_sem,
    take_sem,
    send_sem,
    recv_sem,
    sum_send_sem,
    sum_recv_sem,
    ring_sem,
    plane_sem,
):
    half_points = points // GROUPS
    made, sent = chunk_plan(points)
    lands = (early_ref, mine_ref)
    here = lax.axis_index("space")
    me = lax.axis_index("tblock")
    level = me // 2
    core = lax.rem(me, 2)
    high = here // SIDE
    wide = lax.rem(here, SIDE)

    def peer(dz, dc):
        return lax.rem(level + dz, LEVELS) * 2 + lax.rem(core + dc, 2)

    def plane(dy, dx):
        return lax.rem(high + dy, SIDE) * SIDE + lax.rem(wide + dx, SIDE)

    def signal(sem, **device):
        pl.semaphore_signal(sem, inc=1, device_id=device, device_id_type=MESH)

    rings = [[(0, 1)]] + [
        [(dz, dc) for dz in sorted({far, LEVELS - far}) for dc in (0, 1)]
        for far in range(1, LEVELS // 2 + 1)
    ]
    rings = [rings[1] + rings[0]] + rings[2:]
    peers = [pair for ring in rings[::-1] for pair in ring]

    def take(k, half):
        comp, start, width = made[k]
        return pltpu.make_async_copy(
            series_ref.at[comp, :, pl.ds(half * half_points + start, width)],
            taken_ref.at[k % 2, half, :, pl.ds(0, width)],
            take_sem.at[k % 2, half],
        )

    def send(k, dz, dc):
        group, start, width = sent[k]
        to = peer(dz, dc)
        return pltpu.make_async_remote_copy(
            src_ref=made_ref.at[group, to, :, pl.ds(start, width)],
            dst_ref=lands[group].at[me, :, pl.ds(start, width)],
            send_sem=send_sem.at[k, to],
            recv_sem=recv_sem.at[k, me],
            device_id={"tblock": to},
            device_id_type=MESH,
        )

    def arrival(k, dz, dc):
        group, start, width = sent[k]
        sender = peer(dz, dc)
        return pltpu.make_async_remote_copy(
            src_ref=made_ref.at[group, sender, :, pl.ds(start, width)],
            dst_ref=lands[group].at[sender, :, pl.ds(start, width)],
            send_sem=send_sem.at[k, sender],
            recv_sem=recv_sem.at[k, sender],
            device_id={"tblock": sender},
            device_id_type=MESH,
        )

    def make(k):
        comp, start, width = made[k]
        columns = pl.ds(comp * half_points + start, width)
        for half in range(GROUPS):
            take(k, half).wait()
            spectra = jnp.dot(
                round_ref[...], taken_ref[k % 2, half, :, :width], preferred_element_type=jnp.float32
            )
            made_ref[:, :, pl.ds(half * GROUP_ROWS, GROUP_ROWS), columns] = spectra.astype(
                jnp.bfloat16
            ).reshape(GROUPS, BLOCKS, GROUP_ROWS, width)
            if k + 2 < len(made):
                take(k + 2, half).start()
        for group in range(GROUPS):
            lands[group][me, :, columns] = made_ref[group, me, :, columns]

    table = pltpu.make_async_copy(table_ref, rows_ref, table_sem)
    table.start()
    for half in range(GROUPS):
        take(0, half).start()
    barrier = pltpu.get_barrier_semaphore()
    for dz, dc in rings[0]:
        signal(barrier, tblock=peer(dz, dc))
    sides = [(0, 1), (0, SIDE - 1), (1, 0), (SIDE - 1, 0)]
    for dy, dx in sides:
        signal(barrier, space=plane(dy, dx))
    for half in range(GROUPS):
        take(1, half).start()
    table.wait()
    round_ref[...] = rows_ref[...].astype(jnp.bfloat16)
    make(0)
    pl.semaphore_wait(barrier, len(rings[0]) + len(sides))

    for r, ring in enumerate(rings):
        if r:
            pl.semaphore_wait(ring_sem.at[r - 1, 0], 1)
            pl.semaphore_wait(ring_sem.at[r - 1, 1], 1)
        if r + 1 < len(rings):
            signal(ring_sem.at[r, 0], tblock=peer(1, 0))
            signal(ring_sem.at[r, 1], tblock=peer(LEVELS - 1, 0))
        for dz, dc in ring:
            send(0, dz, dc).start()
        if r == 0:
            signal(plane_sem.at[0], space=plane(0, SIDE - 1))
            make(1)
    for dz, dc in peers:
        send(1, dz, dc).start()
    make(2)
    for dz, dc in peers:
        send(2, dz, dc).start()
    pl.semaphore_wait(plane_sem.at[0], 1)
    signal(plane_sem.at[1], space=plane(1, 0))
    signal(plane_sem.at[2], space=plane(SIDE - 1, 0))
    for k in range(3, len(made)):
        make(k)
    for k in range(3, len(sent)):
        for dz, dc in peers:
            send(k, dz, dc).start()
    pl.semaphore_wait(plane_sem.at[1], 1)
    pl.semaphore_wait(plane_sem.at[2], 1)
    signal(plane_sem.at[3], space=plane(SIDE - 1, 0))
    pl.semaphore_wait(plane_sem.at[3], 1)

    others = range(1, SIDE * SIDE)

    def exchange(group, d, arriving):
        other = lax.rem(here + d, SIDE * SIDE)
        slot = other if arriving else here
        return pltpu.make_async_remote_copy(
            src_ref=packed_ref.at[group, here],
            dst_ref=packed_ref.at[group, slot],
            send_sem=sum_send_sem.at[group, other],
            recv_sem=sum_recv_sem.at[group, slot],
            device_id={"space": other},
            device_id_type=MESH,
        )

    def solve(group):
        opened = False
        for k in range(len(sent)):
            owner, start, width = sent[k]
            if owner != group:
                continue
            for dz, dc in peers:
                arrival(k, dz, dc).wait_recv()
            rows = lands[group][:, :, pl.ds(start, width)].reshape(BLOCKS * ROWS, width)
            part = lax.dot_general(
                rows, rows, (((1,), (1,)), ((), ())), preferred_element_type=jnp.float32
            )
            total_ref[...] = total_ref[...] + part if opened else part
            opened = True
        packed_ref[group, here] = pack_gram(total_ref[...])
        for d in others:
            exchange(group, d, False).start()
        for d in others:
            exchange(group, d, True).wait_recv()
        packed = packed_ref[group, 0]
        for s in others:
            packed = packed + packed_ref[group, s]
        vec_real, vec_imag, energies = leading_modes(packed / scale, gram_ref)
        coef = coefficient_matrix(vec_real, vec_imag, energies, order_ref)
        return coef, jnp.concatenate(energies, axis=0)

    lane = lax.broadcasted_iota(jnp.int32, (MODES, LANES), 1)

    def settle(group, spread):
        narrow = spread
        for f in range(GROUP_BINS):
            to = group * GROUP_BINS + f
            if to != 2 * f:
                narrow = jnp.where(lane == to, pltpu.roll(spread, (to - 2 * f) % LANES, 1), narrow)
        columns = slice(group * GROUP_BINS, (group + 1) * GROUP_BINS)
        energy_ref[:, columns] = narrow[:, columns]

    coef, spread = solve(0)
    settle(0, spread)
    for comp in range(COMPS):

        def put(f, part, half, rows):
            done_ref[f, part, comp, :, pl.ds(half * half_points, half_points)] = rows

        group_modes(coef, early_ref, pl.ds(comp * half_points, half_points), put)

    coef, spread = solve(1)
    coef_ref[...] = coef
    settle(1, spread)

    for k in range(len(sent)):
        for dz, dc in peers:
            send(k, dz, dc).wait_send()
    for group in range(GROUPS):
        for d in others:
            exchange(group, d, False).wait_send()


def modes_kernel(
    coef_ref, mine_ref, done_ref, energy_ref, out_ref, energy_out_ref, held_ref, sem, done_sem
):
    half_points = held_ref.shape[4] // GROUPS
    early = pltpu.make_async_copy(done_ref, out_ref.at[pl.ds(0, GROUP_BINS)], done_sem.at[0])
    early.start()
    energy = pltpu.make_async_copy(energy_ref, energy_out_ref, done_sem.at[1])
    energy.start()

    def late(comp):
        return pltpu.make_async_copy(
            held_ref.at[comp], out_ref.at[pl.ds(GROUP_BINS, GROUP_BINS), :, comp], sem.at[comp]
        )

    for comp in range(COMPS):

        def put(f, part, half, rows):
            held_ref[comp, f, part, :, pl.ds(half * half_points, half_points)] = rows

        group_modes(coef_ref[...], mine_ref, pl.ds(comp * half_points, half_points), put)
        late(comp).start()
    for comp in range(COMPS):
        late(comp).wait()
    early.wait()
    energy.wait()


def local(snapshots, space_count):
    points = snapshots.shape[3]
    width = COMPS * points // GROUPS
    pieces = len(chunk_plan(points)[1])
    series = jnp.transpose(snapshots, (0, 2, 1, 3)).reshape(COMPS, STEPS, points)
    vmem = pl.BlockSpec(memory_space=pltpu.VMEM)
    hbm = pl.BlockSpec(memory_space=pltpu.HBM)
    mine, done, coef, energies = pl.pallas_call(
        functools.partial(spectra_kernel, points, float(COMPS * points * space_count)),
        out_shape=(
            pltpu.VMEM((BLOCKS, ROWS, width), jnp.bfloat16),
            pltpu.VMEM((GROUP_BINS, 2, COMPS, MODES, points), jnp.bfloat16),
            pltpu.VMEM((BINS * 2 * MODES, BLOCKS * ROWS), jnp.bfloat16),
            pltpu.VMEM((MODES, BINS), jnp.float32),
        ),
        in_specs=[hbm, hbm],
        out_specs=(vmem, vmem, vmem, vmem),
        scratch_shapes=[
            pltpu.VMEM((STEPS, STEPS), jnp.float32),
            pltpu.VMEM((STEPS, STEPS), jnp.bfloat16),
            pltpu.VMEM((2, GROUPS, STEPS, points // GROUPS), jnp.bfloat16),
            pltpu.VMEM((GROUPS, BLOCKS, ROWS, width), jnp.bfloat16),
            pltpu.VMEM((BLOCKS, ROWS, width), jnp.bfloat16),
            pltpu.VMEM((BLOCKS * ROWS, BLOCKS * ROWS), jnp.float32),
            pltpu.VMEM((GROUPS, SIDE * SIDE, BLOCKS, LANES), jnp.float32),
            pltpu.VMEM((2, BLOCKS, BLOCKS, LANES), jnp.float32),
            pltpu.VMEM((2, BINS * 2 * MODES, LANES), jnp.float32),
            pltpu.SemaphoreType.DMA,
            pltpu.SemaphoreType.DMA((2, GROUPS)),
            pltpu.SemaphoreType.DMA((pieces, BLOCKS)),
            pltpu.SemaphoreType.DMA((pieces, BLOCKS)),
            pltpu.SemaphoreType.DMA((GROUPS, SIDE * SIDE)),
            pltpu.SemaphoreType.DMA((GROUPS, SIDE * SIDE)),
            pltpu.SemaphoreType.REGULAR((LEVELS // 2 - 1, 2)),
            pltpu.SemaphoreType.REGULAR((4,)),
        ],
        compiler_params=pltpu.CompilerParams(
            collective_id=0, has_side_effects=True, vmem_limit_bytes=VMEM_BYTES
        ),
        cost_estimate=pl.CostEstimate(
            flops=4 * STEPS * STEPS * COMPS * points,
            bytes_accessed=2 * STEPS * COMPS * points,
            transcendentals=0,
        ),
        name="spectra_exchange",
    )(spectral_table(), series)
    modes, energies = pl.pallas_call(
        modes_kernel,
        out_shape=(
            jax.ShapeDtypeStruct((BINS, 2, COMPS, MODES, points), jnp.bfloat16),
            jax.ShapeDtypeStruct((MODES, BINS), jnp.float32),
        ),
        in_specs=[vmem, vmem, vmem, vmem],
        out_specs=(hbm, hbm),
        scratch_shapes=[
            pltpu.VMEM((COMPS, GROUP_BINS, 2, MODES, points), jnp.bfloat16),
            pltpu.SemaphoreType.DMA((COMPS,)),
            pltpu.SemaphoreType.DMA((2,)),
        ],
        compiler_params=pltpu.CompilerParams(vmem_limit_bytes=MODES_VMEM_BYTES),
        cost_estimate=pl.CostEstimate(
            flops=4 * STEPS * BINS * 2 * MODES * COMPS * points,
            bytes_accessed=2 * STEPS * COMPS * points,
            transcendentals=0,
        ),
        name="modes_product",
    )(coef, mine, done, energies)
    return jnp.transpose(modes, (0, 1, 3, 2, 4)), energies.T


def solution(mesh):
    in_specs = (P("tblock", None, None, "space"),)
    out_specs = (P("tblock", None, None, None, "space"), P("tblock", None))
    body = functools.partial(local, space_count=mesh.shape["space"])
    return jax.shard_map(body, mesh=mesh, in_specs=in_specs, out_specs=out_specs, check_vma=False)
```

```python
import functools
import math

import jax
import jax.numpy as jnp
import numpy as np
from jax import lax
from jax.experimental import pallas as pl
from jax.experimental.pallas import tpu as pltpu
from jax.sharding import PartitionSpec as P

MODES = 4
SUBSPACE_ITERS = 6
BLOCKS = 16
STEPS = 256
BINS = 8
ROWS = 2 * BINS
COMPS = 3
GROUPS = 2
GROUP_BINS = BINS // GROUPS
GROUP_ROWS = ROWS // GROUPS
LEVELS = 8
SIDE = 4
LANES = 128
MESH = pl.DeviceIdType.MESH
VMEM_BYTES = 50 * 2**20
MODES_VMEM_BYTES = 16 * 2**20


def spectral_table():
    times = np.arange(STEPS, dtype=np.int32)
    orders = np.arange(1, STEPS // 2 + 1, dtype=np.int32)
    phase = orders[:, None] * times[None, :] % STEPS
    angle = np.float32(2.0 * math.pi / STEPS) * phase.astype(np.float32)
    swing = np.cos(np.float32(2.0 * math.pi / STEPS) * times.astype(np.float32))
    window = np.float32(0.5) - np.float32(0.5) * swing
    scaled = window / np.float32(math.sqrt(0.375 * STEPS))
    rows = np.stack([scaled * np.cos(angle), -scaled * np.sin(angle)], axis=1)
    rows = rows.reshape(BLOCKS, GROUPS, GROUP_ROWS, STEPS).transpose(1, 0, 2, 3)
    return jnp.asarray(rows.reshape(STEPS, STEPS).astype(np.float32))


def chunk_plan(points):
    half = points // GROUPS
    first, second, last = 4 * LANES, 20 * LANES, 8 * LANES
    made = [(0, 0, first), (0, first, second - first), (0, second, half - second)]
    made += [(c, 0, half) for c in range(1, COMPS)]
    sent = [(0, 0, first), (0, first, second - first), (0, second, COMPS * half - second)]
    sent += [(1, 0, COMPS * half - last), (1, COMPS * half - last, last)]
    return made, sent


def pack_gram(total):
    width = total.shape[1]
    cube = total.reshape(BLOCKS, ROWS, width)
    row = lax.broadcasted_iota(jnp.int32, (ROWS, width), 0)
    lane = lax.broadcasted_iota(jnp.int32, (ROWS, width), 1) % ROWS
    same_bin = row // 2 == lane // 2
    same_part = row % 2 == lane % 2
    first = jnp.where(same_bin & same_part, 1.0, 0.0)
    other = jnp.where(same_bin & (row % 2 < lane % 2), 1.0, 0.0)
    other = jnp.where(same_bin & (row % 2 > lane % 2), -1.0, other)
    real = jnp.sum(cube * first[None], axis=1)
    imag = jnp.sum(cube * other[None], axis=1)
    even = lax.broadcasted_iota(jnp.int32, (BLOCKS, width), 1) % 2 == 0
    real = real + pltpu.roll(real, width - 1, 1)
    imag = imag + pltpu.roll(imag, 1, 1)
    both = jnp.where(even, real, imag)
    left, right = both[:, :LANES], both[:, LANES:]
    left = left + pltpu.roll(left, LANES - GROUP_ROWS, 1)
    right = right + pltpu.roll(right, GROUP_ROWS, 1)
    return jnp.where(first_half((BLOCKS, LANES)), left, right)


def first_half(shape):
    return lax.broadcasted_iota(jnp.int32, shape, 1) % ROWS < GROUP_ROWS


def column_sum(value):
    return jnp.sum(value, axis=0, keepdims=True)


def leading_modes(packed, gram_ref):
    even = lax.broadcasted_iota(jnp.int32, (BLOCKS, LANES), 1) % 2 == 0
    low = first_half((BLOCKS, LANES))
    per_half = LANES // ROWS
    for half in range(2):
        if half:
            part = jnp.where(low, pltpu.roll(packed, LANES - GROUP_ROWS, 1), packed)
        else:
            part = jnp.where(low, packed, pltpu.roll(packed, GROUP_ROWS, 1))
        real = jnp.where(even, part, pltpu.roll(part, 1, 1))
        imag = jnp.where(even, pltpu.roll(part, LANES - 1, 1), part)
        for near in range(per_half):
            shift = (LANES - ROWS * near) % LANES
            block = half * per_half + near
            gram_ref[0, block] = real if shift == 0 else pltpu.roll(real, shift, 1)
            gram_ref[1, block] = imag if shift == 0 else pltpu.roll(imag, shift, 1)

    def apply_gram(vec_real, vec_imag):
        out_real = [None] * MODES
        out_imag = [None] * MODES
        for block in range(BLOCKS):
            real = gram_ref[0, block]
            imag = gram_ref[1, block]
            for j in range(MODES):
                row_real = vec_real[j][block : block + 1]
                row_imag = vec_imag[j][block : block + 1]
                term_real = real * row_real - imag * row_imag
                term_imag = real * row_imag + imag * row_real
                out_real[j] = term_real if block == 0 else out_real[j] + term_real
                out_imag[j] = term_imag if block == 0 else out_imag[j] + term_imag
        return out_real, out_imag

    def orthonormal(vec_real, vec_imag):
        vec_real = list(vec_real)
        vec_imag = list(vec_imag)
        for i in range(MODES):
            base_real = vec_real[i]
            base_imag = vec_imag[i]
            square = column_sum(base_real * base_real + base_imag * base_imag)
            inverse = 1.0 / square
            for j in range(i + 1, MODES):
                proj_real = column_sum(base_real * vec_real[j] + base_imag * vec_imag[j]) * inverse
                proj_imag = column_sum(base_real * vec_imag[j] - base_imag * vec_real[j]) * inverse
                vec_real[j] = vec_real[j] - (base_real * proj_real - base_imag * proj_imag)
                vec_imag[j] = vec_imag[j] - (base_real * proj_imag + base_imag * proj_real)
            scale = lax.rsqrt(square)
            vec_real[i] = base_real * scale
            vec_imag[i] = base_imag * scale
        return vec_real, vec_imag

    wide_real = [gram_ref[0, j] for j in range(MODES)]
    wide_imag = [gram_ref[1, j] for j in range(MODES)]
    vec_real, vec_imag = orthonormal(wide_real, wide_imag)

    def sweep(_, carry):
        return orthonormal(*apply_gram(*carry))

    vec_real, vec_imag = lax.fori_loop(1, SUBSPACE_ITERS, sweep, (vec_real, vec_imag))
    wide_real, wide_imag = apply_gram(vec_real, vec_imag)
    energies = [
        column_sum(vec_real[j] * wide_real[j] + vec_imag[j] * wide_imag[j]) for j in range(MODES)
    ]
    return vec_real, vec_imag, energies


def coefficient_matrix(vec_real, vec_imag, energies, order_ref):
    lane = lax.broadcasted_iota(jnp.int32, (BLOCKS, LANES), 1)
    even = lane % 2 == 0
    first = jnp.zeros((BLOCKS, LANES), jnp.float32)
    second = jnp.zeros((BLOCKS, LANES), jnp.float32)
    for j in range(MODES):
        scale = 1.0 / jnp.sqrt(energies[j])
        amp_real = vec_real[j] * scale
        amp_imag = vec_imag[j] * scale
        on_real = jnp.where(even, amp_real, amp_imag)
        on_imag = jnp.where(even, -amp_imag, amp_real)
        if j:
            on_real = pltpu.roll(on_real, ROWS * j, 1)
            on_imag = pltpu.roll(on_imag, ROWS * j, 1)
        here = lane // ROWS == j
        first = jnp.where(here, on_real, first)
        second = jnp.where(here, on_imag, second)
    shape = (BLOCKS, ROWS, LANES)
    row = lax.broadcasted_iota(jnp.int32, shape, 1)
    column = lax.broadcasted_iota(jnp.int32, shape, 2)
    whole = jnp.where(
        row % 2 == 0,
        jnp.broadcast_to(first[:, None, :], shape),
        jnp.broadcast_to(second[:, None, :], shape),
    )
    whole = jnp.where(row // 2 == column % ROWS // 2, whole, 0.0)
    turned = whole.reshape(BLOCKS * ROWS, LANES).T
    for j in range(MODES):
        for half in range(2):
            piece = turned[ROWS * j : ROWS * (j + 1), half * LANES : (half + 1) * LANES]
            order_ref[half, pl.ds(j, ROWS, stride=MODES), :] = piece
    return jnp.concatenate([order_ref[0], order_ref[1]], axis=1).astype(jnp.bfloat16)


def group_modes(coef, mine_ref, columns, put):
    rows = mine_ref[:, :, columns]
    rows = rows.reshape(BLOCKS * ROWS, rows.shape[2])
    modes = jnp.dot(coef, rows, preferred_element_type=jnp.float32).astype(jnp.bfloat16)
    for half in range(GROUPS):
        for f in range(GROUP_BINS):
            for part in range(2):
                start = ((half * GROUP_BINS + f) * 2 + part) * MODES
                put(f, part, half, modes[start : start + MODES])


def spectra_kernel(
    points,
    scale,
    table_ref,
    series_ref,
    mine_ref,
    done_ref,
    coef_ref,
    energy_ref,
    rows_ref,
    round_ref,
    taken_ref,
    made_ref,
    early_ref,
    total_ref,
    packed_ref,
    gram_ref,
    order_ref,
    table_sem,
    take_sem,
    send_sem,
    recv_sem,
    sum_send_sem,
    sum_recv_sem,
    ring_sem,
    plane_sem,
):
    half_points = points // GROUPS
    made, sent = chunk_plan(points)
    lands = (early_ref, mine_ref)
    here = lax.axis_index("space")
    me = lax.axis_index("tblock")
    level = me // 2
    core = lax.rem(me, 2)
    high = here // SIDE
    wide = lax.rem(here, SIDE)

    def peer(dz, dc):
        return lax.rem(level + dz, LEVELS) * 2 + lax.rem(core + dc, 2)

    def plane(dy, dx):
        return lax.rem(high + dy, SIDE) * SIDE + lax.rem(wide + dx, SIDE)

    def signal(sem, **device):
        pl.semaphore_signal(sem, inc=1, device_id=device, device_id_type=MESH)

    rings = [[(0, 1)]] + [
        [(dz, dc) for dz in sorted({far, LEVELS - far}) for dc in (0, 1)]
        for far in range(1, LEVELS // 2 + 1)
    ]
    rings = [rings[1] + rings[0]] + rings[2:]
    peers = [pair for ring in rings[::-1] for pair in ring]

    def take(k, half):
        comp, start, width = made[k]
        return pltpu.make_async_copy(
            series_ref.at[comp, :, pl.ds(half * half_points + start, width)],
            taken_ref.at[k % 2, half, :, pl.ds(0, width)],
            take_sem.at[k % 2, half],
        )

    def send(k, dz, dc):
        group, start, width = sent[k]
        to = peer(dz, dc)
        return pltpu.make_async_remote_copy(
            src_ref=made_ref.at[group, to, :, pl.ds(start, width)],
            dst_ref=lands[group].at[me, :, pl.ds(start, width)],
            send_sem=send_sem.at[k, to],
            recv_sem=recv_sem.at[k, me],
            device_id={"tblock": to},
            device_id_type=MESH,
        )

    def arrival(k, dz, dc):
        group, start, width = sent[k]
        sender = peer(dz, dc)
        return pltpu.make_async_remote_copy(
            src_ref=made_ref.at[group, sender, :, pl.ds(start, width)],
            dst_ref=lands[group].at[sender, :, pl.ds(start, width)],
            send_sem=send_sem.at[k, sender],
            recv_sem=recv_sem.at[k, sender],
            device_id={"tblock": sender},
            device_id_type=MESH,
        )

    def make(k):
        comp, start, width = made[k]
        columns = pl.ds(comp * half_points + start, width)
        for half in range(GROUPS):
            take(k, half).wait()
            spectra = jnp.dot(
                round_ref[...], taken_ref[k % 2, half, :, :width], preferred_element_type=jnp.float32
            )
            made_ref[:, :, pl.ds(half * GROUP_ROWS, GROUP_ROWS), columns] = spectra.astype(
                jnp.bfloat16
            ).reshape(GROUPS, BLOCKS, GROUP_ROWS, width)
            if k + 2 < len(made):
                take(k + 2, half).start()
        for group in range(GROUPS):
            lands[group][me, :, columns] = made_ref[group, me, :, columns]

    table = pltpu.make_async_copy(table_ref, rows_ref, table_sem)
    table.start()
    for half in range(GROUPS):
        take(0, half).start()
    barrier = pltpu.get_barrier_semaphore()
    for dz, dc in rings[0]:
        signal(barrier, tblock=peer(dz, dc))
    sides = [(0, 1), (0, SIDE - 1), (1, 0), (SIDE - 1, 0)]
    for dy, dx in sides:
        signal(barrier, space=plane(dy, dx))
    for half in range(GROUPS):
        take(1, half).start()
    table.wait()
    round_ref[...] = rows_ref[...].astype(jnp.bfloat16)
    make(0)
    pl.semaphore_wait(barrier, len(rings[0]) + len(sides))

    for r, ring in enumerate(rings):
        if r:
            pl.semaphore_wait(ring_sem.at[r - 1, 0], 1)
            pl.semaphore_wait(ring_sem.at[r - 1, 1], 1)
        if r + 1 < len(rings):
            signal(ring_sem.at[r, 0], tblock=peer(1, 0))
            signal(ring_sem.at[r, 1], tblock=peer(LEVELS - 1, 0))
        for dz, dc in ring:
            send(0, dz, dc).start()
        if r == 0:
            signal(plane_sem.at[0], space=plane(0, SIDE - 1))
            make(1)
        for dz, dc in ring:
            send(1, dz, dc).start()
    pl.semaphore_wait(plane_sem.at[0], 1)
    signal(plane_sem.at[1], space=plane(1, 0))
    signal(plane_sem.at[2], space=plane(SIDE - 1, 0))
    for k in range(2, len(made)):
        make(k)
    for k in range(2, len(sent)):
        for dz, dc in peers:
            send(k, dz, dc).start()
    pl.semaphore_wait(plane_sem.at[1], 1)
    pl.semaphore_wait(plane_sem.at[2], 1)
    signal(plane_sem.at[3], space=plane(SIDE - 1, 0))
    pl.semaphore_wait(plane_sem.at[3], 1)

    hops = (0, 1, 2, 1)
    others = [(dy, dx) for dy in range(SIDE) for dx in range(SIDE)][1:]
    others.sort(key=lambda step: -hops[step[0]] - hops[step[1]])

    def exchange(group, step, arriving):
        other = plane(*step)
        slot = other if arriving else here
        return pltpu.make_async_remote_copy(
            src_ref=packed_ref.at[group, here],
            dst_ref=packed_ref.at[group, slot],
            send_sem=sum_send_sem.at[group, other],
            recv_sem=sum_recv_sem.at[group, slot],
            device_id={"space": other},
            device_id_type=MESH,
        )

    def solve(group):
        opened = False
        for k in range(len(sent)):
            owner, start, width = sent[k]
            if owner != group:
                continue
            for dz, dc in peers:
                arrival(k, dz, dc).wait_recv()
            rows = lands[group][:, :, pl.ds(start, width)].reshape(BLOCKS * ROWS, width)
            part = lax.dot_general(
                rows, rows, (((1,), (1,)), ((), ())), preferred_element_type=jnp.float32
            )
            total_ref[...] = total_ref[...] + part if opened else part
            opened = True
        packed_ref[group, here] = pack_gram(total_ref[...])
        for d in others:
            exchange(group, d, False).start()
        for d in others:
            exchange(group, d, True).wait_recv()
        packed = packed_ref[group, 0]
        for s in range(1, SIDE * SIDE):
            packed = packed + packed_ref[group, s]
        vec_real, vec_imag, energies = leading_modes(packed / scale, gram_ref)
        coef = coefficient_matrix(vec_real, vec_imag, energies, order_ref)
        return coef, jnp.concatenate(energies, axis=0)

    lane = lax.broadcasted_iota(jnp.int32, (MODES, LANES), 1)

    def settle(group, spread):
        narrow = spread
        for f in range(GROUP_BINS):
            to = group * GROUP_BINS + f
            if to != 2 * f:
                narrow = jnp.where(lane == to, pltpu.roll(spread, (to - 2 * f) % LANES, 1), narrow)
        columns = slice(group * GROUP_BINS, (group + 1) * GROUP_BINS)
        energy_ref[:, columns] = narrow[:, columns]

    coef, spread = solve(0)
    settle(0, spread)
    for comp in range(COMPS):

        def put(f, part, half, rows):
            done_ref[f, part, comp, :, pl.ds(half * half_points, half_points)] = rows

        group_modes(coef, early_ref, pl.ds(comp * half_points, half_points), put)

    coef, spread = solve(1)
    coef_ref[...] = coef
    settle(1, spread)

    for k in range(len(sent)):
        for dz, dc in peers:
            send(k, dz, dc).wait_send()
    for group in range(GROUPS):
        for d in others:
            exchange(group, d, False).wait_send()


def modes_kernel(
    coef_ref, mine_ref, done_ref, energy_ref, out_ref, energy_out_ref, held_ref, sem, done_sem
):
    half_points = held_ref.shape[4] // GROUPS
    early = pltpu.make_async_copy(done_ref, out_ref.at[pl.ds(0, GROUP_BINS)], done_sem.at[0])
    early.start()
    energy = pltpu.make_async_copy(energy_ref, energy_out_ref, done_sem.at[1])
    energy.start()

    def late(comp):
        return pltpu.make_async_copy(
            held_ref.at[comp], out_ref.at[pl.ds(GROUP_BINS, GROUP_BINS), :, comp], sem.at[comp]
        )

    for comp in range(COMPS):

        def put(f, part, half, rows):
            held_ref[comp, f, part, :, pl.ds(half * half_points, half_points)] = rows

        group_modes(coef_ref[...], mine_ref, pl.ds(comp * half_points, half_points), put)
        late(comp).start()
    for comp in range(COMPS):
        late(comp).wait()
    early.wait()
    energy.wait()


def local(snapshots, space_count):
    points = snapshots.shape[3]
    width = COMPS * points // GROUPS
    pieces = len(chunk_plan(points)[1])
    series = jnp.transpose(snapshots, (0, 2, 1, 3)).reshape(COMPS, STEPS, points)
    vmem = pl.BlockSpec(memory_space=pltpu.VMEM)
    hbm = pl.BlockSpec(memory_space=pltpu.HBM)
    mine, done, coef, energies = pl.pallas_call(
        functools.partial(spectra_kernel, points, float(COMPS * points * space_count)),
        out_shape=(
            pltpu.VMEM((BLOCKS, ROWS, width), jnp.bfloat16),
            pltpu.VMEM((GROUP_BINS, 2, COMPS, MODES, points), jnp.bfloat16),
            pltpu.VMEM((BINS * 2 * MODES, BLOCKS * ROWS), jnp.bfloat16),
            pltpu.VMEM((MODES, BINS), jnp.float32),
        ),
        in_specs=[hbm, hbm],
        out_specs=(vmem, vmem, vmem, vmem),
        scratch_shapes=[
            pltpu.VMEM((STEPS, STEPS), jnp.float32),
            pltpu.VMEM((STEPS, STEPS), jnp.bfloat16),
            pltpu.VMEM((2, GROUPS, STEPS, points // GROUPS), jnp.bfloat16),
            pltpu.VMEM((GROUPS, BLOCKS, ROWS, width), jnp.bfloat16),
            pltpu.VMEM((BLOCKS, ROWS, width), jnp.bfloat16),
            pltpu.VMEM((BLOCKS * ROWS, BLOCKS * ROWS), jnp.float32),
            pltpu.VMEM((GROUPS, SIDE * SIDE, BLOCKS, LANES), jnp.float32),
            pltpu.VMEM((2, BLOCKS, BLOCKS, LANES), jnp.float32),
            pltpu.VMEM((2, BINS * 2 * MODES, LANES), jnp.float32),
            pltpu.SemaphoreType.DMA,
            pltpu.SemaphoreType.DMA((2, GROUPS)),
            pltpu.SemaphoreType.DMA((pieces, BLOCKS)),
            pltpu.SemaphoreType.DMA((pieces, BLOCKS)),
            pltpu.SemaphoreType.DMA((GROUPS, SIDE * SIDE)),
            pltpu.SemaphoreType.DMA((GROUPS, SIDE * SIDE)),
            pltpu.SemaphoreType.REGULAR((LEVELS // 2 - 1, 2)),
            pltpu.SemaphoreType.REGULAR((4,)),
        ],
        compiler_params=pltpu.CompilerParams(
            collective_id=0, has_side_effects=True, vmem_limit_bytes=VMEM_BYTES
        ),
        cost_estimate=pl.CostEstimate(
            flops=4 * STEPS * STEPS * COMPS * points,
            bytes_accessed=2 * STEPS * COMPS * points,
            transcendentals=0,
        ),
        name="spectra_exchange",
    )(spectral_table(), series)
    modes, energies = pl.pallas_call(
        modes_kernel,
        out_shape=(
            jax.ShapeDtypeStruct((BINS, 2, COMPS, MODES, points), jnp.bfloat16),
            jax.ShapeDtypeStruct((MODES, BINS), jnp.float32),
        ),
        in_specs=[vmem, vmem, vmem, vmem],
        out_specs=(hbm, hbm),
        scratch_shapes=[
            pltpu.VMEM((COMPS, GROUP_BINS, 2, MODES, points), jnp.bfloat16),
            pltpu.SemaphoreType.DMA((COMPS,)),
            pltpu.SemaphoreType.DMA((2,)),
        ],
        compiler_params=pltpu.CompilerParams(vmem_limit_bytes=MODES_VMEM_BYTES),
        cost_estimate=pl.CostEstimate(
            flops=4 * STEPS * BINS * 2 * MODES * COMPS * points,
            bytes_accessed=2 * STEPS * COMPS * points,
            transcendentals=0,
        ),
        name="modes_product",
    )(coef, mine, done, energies)
    return jnp.transpose(modes, (0, 1, 3, 2, 4)), energies.T


def solution(mesh):
    in_specs = (P("tblock", None, None, "space"),)
    out_specs = (P("tblock", None, None, None, "space"), P("tblock", None))
    body = functools.partial(local, space_count=mesh.shape["space"])
    return jax.shard_map(body, mesh=mesh, in_specs=in_specs, out_specs=out_specs, check_vma=False)
```

```python
import functools
import math

import jax
import jax.numpy as jnp
import numpy as np
from jax import lax
from jax.experimental import pallas as pl
from jax.experimental.pallas import tpu as pltpu
from jax.sharding import PartitionSpec as P

MODES = 4
SUBSPACE_ITERS = 6
BLOCKS = 16
STEPS = 256
BINS = 8
ROWS = 2 * BINS
COMPS = 3
GROUPS = 2
GROUP_BINS = BINS // GROUPS
GROUP_ROWS = ROWS // GROUPS
LEVELS = 8
SIDE = 4
LANES = 128
MESH = pl.DeviceIdType.MESH
VMEM_BYTES = 50 * 2**20
MODES_VMEM_BYTES = 16 * 2**20


def spectral_table():
    times = np.arange(STEPS, dtype=np.int32)
    orders = np.arange(1, STEPS // 2 + 1, dtype=np.int32)
    phase = orders[:, None] * times[None, :] % STEPS
    angle = np.float32(2.0 * math.pi / STEPS) * phase.astype(np.float32)
    swing = np.cos(np.float32(2.0 * math.pi / STEPS) * times.astype(np.float32))
    window = np.float32(0.5) - np.float32(0.5) * swing
    scaled = window / np.float32(math.sqrt(0.375 * STEPS))
    rows = np.stack([scaled * np.cos(angle), -scaled * np.sin(angle)], axis=1)
    rows = rows.reshape(BLOCKS, GROUPS, GROUP_ROWS, STEPS).transpose(1, 0, 2, 3)
    return jnp.asarray(rows.reshape(STEPS, STEPS).astype(np.float32))


def chunk_plan(points):
    half = points // GROUPS
    first, second, last = 4 * LANES, 20 * LANES, 8 * LANES
    made = [(0, 0, first), (0, first, second - first), (0, second, half - second)]
    made += [(c, 0, half) for c in range(1, COMPS)]
    sent = [(0, 0, first), (0, first, second - first), (0, second, COMPS * half - second)]
    sent += [(1, 0, COMPS * half - last), (1, COMPS * half - last, last)]
    return made, sent


def pack_gram(total):
    width = total.shape[1]
    cube = total.reshape(BLOCKS, ROWS, width)
    row = lax.broadcasted_iota(jnp.int32, (ROWS, width), 0)
    lane = lax.broadcasted_iota(jnp.int32, (ROWS, width), 1) % ROWS
    same_bin = row // 2 == lane // 2
    same_part = row % 2 == lane % 2
    first = jnp.where(same_bin & same_part, 1.0, 0.0)
    other = jnp.where(same_bin & (row % 2 < lane % 2), 1.0, 0.0)
    other = jnp.where(same_bin & (row % 2 > lane % 2), -1.0, other)
    real = jnp.sum(cube * first[None], axis=1)
    imag = jnp.sum(cube * other[None], axis=1)
    even = lax.broadcasted_iota(jnp.int32, (BLOCKS, width), 1) % 2 == 0
    real = real + pltpu.roll(real, width - 1, 1)
    imag = imag + pltpu.roll(imag, 1, 1)
    both = jnp.where(even, real, imag)
    left, right = both[:, :LANES], both[:, LANES:]
    left = left + pltpu.roll(left, LANES - GROUP_ROWS, 1)
    right = right + pltpu.roll(right, GROUP_ROWS, 1)
    return jnp.where(first_half((BLOCKS, LANES)), left, right)


def first_half(shape):
    return lax.broadcasted_iota(jnp.int32, shape, 1) % ROWS < GROUP_ROWS


def column_sum(value):
    return jnp.sum(value, axis=0, keepdims=True)


def leading_modes(packed, gram_ref):
    even = lax.broadcasted_iota(jnp.int32, (BLOCKS, LANES), 1) % 2 == 0
    low = first_half((BLOCKS, LANES))
    per_half = LANES // ROWS
    for half in range(2):
        if half:
            part = jnp.where(low, pltpu.roll(packed, LANES - GROUP_ROWS, 1), packed)
        else:
            part = jnp.where(low, packed, pltpu.roll(packed, GROUP_ROWS, 1))
        real = jnp.where(even, part, pltpu.roll(part, 1, 1))
        imag = jnp.where(even, pltpu.roll(part, LANES - 1, 1), part)
        for near in range(per_half):
            shift = (LANES - ROWS * near) % LANES
            block = half * per_half + near
            gram_ref[0, block] = real if shift == 0 else pltpu.roll(real, shift, 1)
            gram_ref[1, block] = imag if shift == 0 else pltpu.roll(imag, shift, 1)

    def apply_gram(vec_real, vec_imag):
        out_real = [None] * MODES
        out_imag = [None] * MODES
        for block in range(BLOCKS):
            real = gram_ref[0, block]
            imag = gram_ref[1, block]
            for j in range(MODES):
                row_real = vec_real[j][block : block + 1]
                row_imag = vec_imag[j][block : block + 1]
                term_real = real * row_real - imag * row_imag
                term_imag = real * row_imag + imag * row_real
                out_real[j] = term_real if block == 0 else out_real[j] + term_real
                out_imag[j] = term_imag if block == 0 else out_imag[j] + term_imag
        return out_real, out_imag

    def orthonormal(vec_real, vec_imag):
        vec_real = list(vec_real)
        vec_imag = list(vec_imag)
        for i in range(MODES):
            base_real = vec_real[i]
            base_imag = vec_imag[i]
            square = column_sum(base_real * base_real + base_imag * base_imag)
            inverse = 1.0 / square
            for j in range(i + 1, MODES):
                proj_real = column_sum(base_real * vec_real[j] + base_imag * vec_imag[j]) * inverse
                proj_imag = column_sum(base_real * vec_imag[j] - base_imag * vec_real[j]) * inverse
                vec_real[j] = vec_real[j] - (base_real * proj_real - base_imag * proj_imag)
                vec_imag[j] = vec_imag[j] - (base_real * proj_imag + base_imag * proj_real)
            scale = lax.rsqrt(square)
            vec_real[i] = base_real * scale
            vec_imag[i] = base_imag * scale
        return vec_real, vec_imag

    wide_real = [gram_ref[0, j] for j in range(MODES)]
    wide_imag = [gram_ref[1, j] for j in range(MODES)]
    vec_real, vec_imag = orthonormal(wide_real, wide_imag)

    def sweep(_, carry):
        return orthonormal(*apply_gram(*carry))

    vec_real, vec_imag = lax.fori_loop(1, SUBSPACE_ITERS, sweep, (vec_real, vec_imag))
    wide_real, wide_imag = apply_gram(vec_real, vec_imag)
    energies = [
        column_sum(vec_real[j] * wide_real[j] + vec_imag[j] * wide_imag[j]) for j in range(MODES)
    ]
    return vec_real, vec_imag, energies


def coefficient_matrix(vec_real, vec_imag, energies, order_ref):
    lane = lax.broadcasted_iota(jnp.int32, (BLOCKS, LANES), 1)
    even = lane % 2 == 0
    first = jnp.zeros((BLOCKS, LANES), jnp.float32)
    second = jnp.zeros((BLOCKS, LANES), jnp.float32)
    for j in range(MODES):
        scale = 1.0 / jnp.sqrt(energies[j])
        amp_real = vec_real[j] * scale
        amp_imag = vec_imag[j] * scale
        on_real = jnp.where(even, amp_real, amp_imag)
        on_imag = jnp.where(even, -amp_imag, amp_real)
        if j:
            on_real = pltpu.roll(on_real, ROWS * j, 1)
            on_imag = pltpu.roll(on_imag, ROWS * j, 1)
        here = lane // ROWS == j
        first = jnp.where(here, on_real, first)
        second = jnp.where(here, on_imag, second)
    shape = (BLOCKS, ROWS, LANES)
    row = lax.broadcasted_iota(jnp.int32, shape, 1)
    column = lax.broadcasted_iota(jnp.int32, shape, 2)
    whole = jnp.where(
        row % 2 == 0,
        jnp.broadcast_to(first[:, None, :], shape),
        jnp.broadcast_to(second[:, None, :], shape),
    )
    whole = jnp.where(row // 2 == column % ROWS // 2, whole, 0.0)
    turned = whole.reshape(BLOCKS * ROWS, LANES).T
    for j in range(MODES):
        for half in range(2):
            piece = turned[ROWS * j : ROWS * (j + 1), half * LANES : (half + 1) * LANES]
            order_ref[half, pl.ds(j, ROWS, stride=MODES), :] = piece
    return jnp.concatenate([order_ref[0], order_ref[1]], axis=1).astype(jnp.bfloat16)


def group_modes(coef, mine_ref, columns, put):
    rows = mine_ref[:, :, columns]
    rows = rows.reshape(BLOCKS * ROWS, rows.shape[2])
    modes = jnp.dot(coef, rows, preferred_element_type=jnp.float32).astype(jnp.bfloat16)
    for half in range(GROUPS):
        for f in range(GROUP_BINS):
            for part in range(2):
                start = ((half * GROUP_BINS + f) * 2 + part) * MODES
                put(f, part, half, modes[start : start + MODES])


def spectra_kernel(
    points,
    scale,
    table_ref,
    series_ref,
    mine_ref,
    done_ref,
    coef_ref,
    energy_ref,
    rows_ref,
    round_ref,
    taken_ref,
    made_ref,
    early_ref,
    total_ref,
    packed_ref,
    gram_ref,
    order_ref,
    table_sem,
    take_sem,
    send_sem,
    recv_sem,
    sum_send_sem,
    sum_recv_sem,
    ring_sem,
    plane_sem,
):
    half_points = points // GROUPS
    made, sent = chunk_plan(points)
    lands = (early_ref, mine_ref)
    here = lax.axis_index("space")
    me = lax.axis_index("tblock")
    level = me // 2
    core = lax.rem(me, 2)
    high = here // SIDE
    wide = lax.rem(here, SIDE)

    def peer(dz, dc):
        return lax.rem(level + dz, LEVELS) * 2 + lax.rem(core + dc, 2)

    def plane(dy, dx):
        return lax.rem(high + dy, SIDE) * SIDE + lax.rem(wide + dx, SIDE)

    def signal(sem, **device):
        pl.semaphore_signal(sem, inc=1, device_id=device, device_id_type=MESH)

    rings = [[(0, 1)]] + [
        [(dz, dc) for dz in sorted({far, LEVELS - far}) for dc in (0, 1)]
        for far in range(1, LEVELS // 2 + 1)
    ]
    rings = [rings[1] + rings[0]] + rings[2:]
    peers = [pair for ring in rings[::-1] for pair in ring]

    def take(k, half):
        comp, start, width = made[k]
        return pltpu.make_async_copy(
            series_ref.at[comp, :, pl.ds(half * half_points + start, width)],
            taken_ref.at[k % 2, half, :, pl.ds(0, width)],
            take_sem.at[k % 2, half],
        )

    def send(k, dz, dc):
        group, start, width = sent[k]
        to = peer(dz, dc)
        return pltpu.make_async_remote_copy(
            src_ref=made_ref.at[group, to, :, pl.ds(start, width)],
            dst_ref=lands[group].at[me, :, pl.ds(start, width)],
            send_sem=send_sem.at[k],
            recv_sem=recv_sem.at[k],
            device_id={"tblock": to},
            device_id_type=MESH,
        )

    def whole(k):
        group, start, width = sent[k]
        part = lands[group].at[pl.ds(0, BLOCKS - 1), :, pl.ds(start, width)]
        return pltpu.make_async_remote_copy(
            src_ref=part,
            dst_ref=part,
            send_sem=send_sem.at[k],
            recv_sem=recv_sem.at[k],
            device_id={"tblock": peer(1, 0)},
            device_id_type=MESH,
        )

    def make(k):
        comp, start, width = made[k]
        columns = pl.ds(comp * half_points + start, width)
        for half in range(GROUPS):
            take(k, half).wait()
            spectra = jnp.dot(
                round_ref[...], taken_ref[k % 2, half, :, :width], preferred_element_type=jnp.float32
            )
            made_ref[:, :, pl.ds(half * GROUP_ROWS, GROUP_ROWS), columns] = spectra.astype(
                jnp.bfloat16
            ).reshape(GROUPS, BLOCKS, GROUP_ROWS, width)
            if k + 2 < len(made):
                take(k + 2, half).start()
        for group in range(GROUPS):
            lands[group][me, :, columns] = made_ref[group, me, :, columns]

    table = pltpu.make_async_copy(table_ref, rows_ref, table_sem)
    table.start()
    for half in range(GROUPS):
        take(0, half).start()
    barrier = pltpu.get_barrier_semaphore()
    for dz, dc in rings[0]:
        signal(barrier, tblock=peer(dz, dc))
    sides = [(0, 1), (0, SIDE - 1), (1, 0), (SIDE - 1, 0)]
    for dy, dx in sides:
        signal(barrier, space=plane(dy, dx))
    for half in range(GROUPS):
        take(1, half).start()
    table.wait()
    round_ref[...] = rows_ref[...].astype(jnp.bfloat16)
    make(0)
    pl.semaphore_wait(barrier, len(rings[0]) + len(sides))

    for r, ring in enumerate(rings):
        if r:
            pl.semaphore_wait(ring_sem.at[r - 1, 0], 1)
            pl.semaphore_wait(ring_sem.at[r - 1, 1], 1)
        if r + 1 < len(rings):
            signal(ring_sem.at[r, 0], tblock=peer(1, 0))
            signal(ring_sem.at[r, 1], tblock=peer(LEVELS - 1, 0))
        for dz, dc in ring:
            send(0, dz, dc).start()
        if r == 0:
            signal(plane_sem.at[0], space=plane(0, SIDE - 1))
            make(1)
        for dz, dc in ring:
            send(1, dz, dc).start()
    pl.semaphore_wait(plane_sem.at[0], 1)
    signal(plane_sem.at[1], space=plane(1, 0))
    signal(plane_sem.at[2], space=plane(SIDE - 1, 0))
    for k in range(2, len(made)):
        make(k)
    for k in range(2, len(sent)):
        for dz, dc in peers:
            send(k, dz, dc).start()
    pl.semaphore_wait(plane_sem.at[1], 1)
    pl.semaphore_wait(plane_sem.at[2], 1)
    signal(plane_sem.at[3], space=plane(SIDE - 1, 0))
    pl.semaphore_wait(plane_sem.at[3], 1)

    hops = (0, 1, 2, 1)
    others = [(dy, dx) for dy in range(SIDE) for dx in range(SIDE)][1:]
    others.sort(key=lambda step: -hops[step[0]] - hops[step[1]])

    def exchange(group, step):
        return pltpu.make_async_remote_copy(
            src_ref=packed_ref.at[group, here],
            dst_ref=packed_ref.at[group, here],
            send_sem=sum_send_sem.at[group],
            recv_sem=sum_recv_sem.at[group],
            device_id={"space": plane(*step)},
            device_id_type=MESH,
        )

    def whole_exchange(group):
        part = packed_ref.at[group, pl.ds(0, SIDE * SIDE - 1)]
        return pltpu.make_async_remote_copy(
            src_ref=part,
            dst_ref=part,
            send_sem=sum_send_sem.at[group],
            recv_sem=sum_recv_sem.at[group],
            device_id={"space": plane(0, 1)},
            device_id_type=MESH,
        )

    def solve(group):
        opened = False
        for k in range(len(sent)):
            owner, start, width = sent[k]
            if owner != group:
                continue
            whole(k).wait_recv()
            rows = lands[group][:, :, pl.ds(start, width)].reshape(BLOCKS * ROWS, width)
            part = lax.dot_general(
                rows, rows, (((1,), (1,)), ((), ())), preferred_element_type=jnp.float32
            )
            total_ref[...] = total_ref[...] + part if opened else part
            opened = True
        packed_ref[group, here] = pack_gram(total_ref[...])
        for d in others:
            exchange(group, d).start()
        for k in range(len(sent)):
            if sent[k][0] == group:
                whole(k).wait_send()
        whole_exchange(group).wait_recv()
        packed = packed_ref[group, 0]
        for s in range(1, SIDE * SIDE):
            packed = packed + packed_ref[group, s]
        vec_real, vec_imag, energies = leading_modes(packed / scale, gram_ref)
        coef = coefficient_matrix(vec_real, vec_imag, energies, order_ref)
        return coef, jnp.concatenate(energies, axis=0)

    lane = lax.broadcasted_iota(jnp.int32, (MODES, LANES), 1)

    def settle(group, spread):
        narrow = spread
        for f in range(GROUP_BINS):
            to = group * GROUP_BINS + f
            if to != 2 * f:
                narrow = jnp.where(lane == to, pltpu.roll(spread, (to - 2 * f) % LANES, 1), narrow)
        columns = slice(group * GROUP_BINS, (group + 1) * GROUP_BINS)
        energy_ref[:, columns] = narrow[:, columns]

    coef, spread = solve(0)
    whole_exchange(0).wait_send()
    settle(0, spread)
    for comp in range(COMPS):

        def put(f, part, half, rows):
            done_ref[f, part, comp, :, pl.ds(half * half_points, half_points)] = rows

        group_modes(coef, early_ref, pl.ds(comp * half_points, half_points), put)

    coef, spread = solve(1)
    coef_ref[...] = coef
    settle(1, spread)

    whole_exchange(1).wait_send()


def modes_kernel(
    coef_ref, mine_ref, done_ref, energy_ref, out_ref, energy_out_ref, held_ref, sem, done_sem
):
    half_points = held_ref.shape[4] // GROUPS
    early = pltpu.make_async_copy(done_ref, out_ref.at[pl.ds(0, GROUP_BINS)], done_sem.at[0])
    early.start()
    energy = pltpu.make_async_copy(energy_ref, energy_out_ref, done_sem.at[1])
    energy.start()

    def late(comp):
        return pltpu.make_async_copy(
            held_ref.at[comp], out_ref.at[pl.ds(GROUP_BINS, GROUP_BINS), :, comp], sem.at[comp]
        )

    for comp in range(COMPS):

        def put(f, part, half, rows):
            held_ref[comp, f, part, :, pl.ds(half * half_points, half_points)] = rows

        group_modes(coef_ref[...], mine_ref, pl.ds(comp * half_points, half_points), put)
        late(comp).start()
    for comp in range(COMPS):
        late(comp).wait()
    early.wait()
    energy.wait()


def local(snapshots, space_count):
    points = snapshots.shape[3]
    width = COMPS * points // GROUPS
    pieces = len(chunk_plan(points)[1])
    series = jnp.transpose(snapshots, (0, 2, 1, 3)).reshape(COMPS, STEPS, points)
    vmem = pl.BlockSpec(memory_space=pltpu.VMEM)
    hbm = pl.BlockSpec(memory_space=pltpu.HBM)
    mine, done, coef, energies = pl.pallas_call(
        functools.partial(spectra_kernel, points, float(COMPS * points * space_count)),
        out_shape=(
            pltpu.VMEM((BLOCKS, ROWS, width), jnp.bfloat16),
            pltpu.VMEM((GROUP_BINS, 2, COMPS, MODES, points), jnp.bfloat16),
            pltpu.VMEM((BINS * 2 * MODES, BLOCKS * ROWS), jnp.bfloat16),
            pltpu.VMEM((MODES, BINS), jnp.float32),
        ),
        in_specs=[hbm, hbm],
        out_specs=(vmem, vmem, vmem, vmem),
        scratch_shapes=[
            pltpu.VMEM((STEPS, STEPS), jnp.float32),
            pltpu.VMEM((STEPS, STEPS), jnp.bfloat16),
            pltpu.VMEM((2, GROUPS, STEPS, points // GROUPS), jnp.bfloat16),
            pltpu.VMEM((GROUPS, BLOCKS, ROWS, width), jnp.bfloat16),
            pltpu.VMEM((BLOCKS, ROWS, width), jnp.bfloat16),
            pltpu.VMEM((BLOCKS * ROWS, BLOCKS * ROWS), jnp.float32),
            pltpu.VMEM((GROUPS, SIDE * SIDE, BLOCKS, LANES), jnp.float32),
            pltpu.VMEM((2, BLOCKS, BLOCKS, LANES), jnp.float32),
            pltpu.VMEM((2, BINS * 2 * MODES, LANES), jnp.float32),
            pltpu.SemaphoreType.DMA,
            pltpu.SemaphoreType.DMA((2, GROUPS)),
            pltpu.SemaphoreType.DMA((pieces,)),
            pltpu.SemaphoreType.DMA((pieces,)),
            pltpu.SemaphoreType.DMA((GROUPS,)),
            pltpu.SemaphoreType.DMA((GROUPS,)),
            pltpu.SemaphoreType.REGULAR((LEVELS // 2 - 1, 2)),
            pltpu.SemaphoreType.REGULAR((4,)),
        ],
        compiler_params=pltpu.CompilerParams(
            collective_id=0, has_side_effects=True, vmem_limit_bytes=VMEM_BYTES
        ),
        cost_estimate=pl.CostEstimate(
            flops=4 * STEPS * STEPS * COMPS * points,
            bytes_accessed=2 * STEPS * COMPS * points,
            transcendentals=0,
        ),
        name="spectra_exchange",
    )(spectral_table(), series)
    modes, energies = pl.pallas_call(
        modes_kernel,
        out_shape=(
            jax.ShapeDtypeStruct((BINS, 2, COMPS, MODES, points), jnp.bfloat16),
            jax.ShapeDtypeStruct((MODES, BINS), jnp.float32),
        ),
        in_specs=[vmem, vmem, vmem, vmem],
        out_specs=(hbm, hbm),
        scratch_shapes=[
            pltpu.VMEM((COMPS, GROUP_BINS, 2, MODES, points), jnp.bfloat16),
            pltpu.SemaphoreType.DMA((COMPS,)),
            pltpu.SemaphoreType.DMA((2,)),
        ],
        compiler_params=pltpu.CompilerParams(vmem_limit_bytes=MODES_VMEM_BYTES),
        cost_estimate=pl.CostEstimate(
            flops=4 * STEPS * BINS * 2 * MODES * COMPS * points,
            bytes_accessed=2 * STEPS * COMPS * points,
            transcendentals=0,
        ),
        name="modes_product",
    )(coef, mine, done, energies)
    return jnp.transpose(modes, (0, 1, 3, 2, 4)), energies.T


def solution(mesh):
    in_specs = (P("tblock", None, None, "space"),)
    out_specs = (P("tblock", None, None, None, "space"), P("tblock", None))
    body = functools.partial(local, space_count=mesh.shape["space"])
    return jax.shard_map(body, mesh=mesh, in_specs=in_specs, out_specs=out_specs, check_vma=False)
```

```python
import functools
import math

import jax
import jax.numpy as jnp
import numpy as np
from jax import lax
from jax.experimental import pallas as pl
from jax.experimental.pallas import tpu as pltpu
from jax.sharding import PartitionSpec as P

MODES = 4
SUBSPACE_ITERS = 6
BLOCKS = 16
STEPS = 256
BINS = 8
ROWS = 2 * BINS
COMPS = 3
GROUPS = 2
GROUP_BINS = BINS // GROUPS
GROUP_ROWS = ROWS // GROUPS
LEVELS = 8
MARGIN = 8
SIDE = 4
LANES = 128
MESH = pl.DeviceIdType.MESH
VMEM_BYTES = 50 * 2**20
MODES_VMEM_BYTES = 16 * 2**20


def spectral_table():
    times = np.arange(STEPS, dtype=np.int32)
    orders = np.arange(1, STEPS // 2 + 1, dtype=np.int32)
    phase = orders[:, None] * times[None, :] % STEPS
    angle = np.float32(2.0 * math.pi / STEPS) * phase.astype(np.float32)
    swing = np.cos(np.float32(2.0 * math.pi / STEPS) * times.astype(np.float32))
    window = np.float32(0.5) - np.float32(0.5) * swing
    scaled = window / np.float32(math.sqrt(0.375 * STEPS))
    rows = np.stack([scaled * np.cos(angle), -scaled * np.sin(angle)], axis=1)
    rows = rows.reshape(BLOCKS, GROUPS, GROUP_ROWS, STEPS).transpose(1, 0, 2, 3)
    return jnp.asarray(rows.reshape(STEPS, STEPS).astype(np.float32))


def chunk_plan(points):
    half = points // GROUPS
    first, second, last = 4 * LANES, 20 * LANES, 8 * LANES
    made = [(0, 0, first), (0, first, second - first), (0, second, half - second)]
    made += [(c, 0, half) for c in range(1, COMPS)]
    sent = [(0, 0, first), (0, first, second - first), (0, second, COMPS * half - second)]
    sent += [(1, 0, COMPS * half - last), (1, COMPS * half - last, last)]
    return made, sent


def pack_gram(total):
    width = total.shape[1]
    cube = total.reshape(BLOCKS, ROWS, width)
    row = lax.broadcasted_iota(jnp.int32, (ROWS, width), 0)
    lane = lax.broadcasted_iota(jnp.int32, (ROWS, width), 1) % ROWS
    same_bin = row // 2 == lane // 2
    same_part = row % 2 == lane % 2
    first = jnp.where(same_bin & same_part, 1.0, 0.0)
    other = jnp.where(same_bin & (row % 2 < lane % 2), 1.0, 0.0)
    other = jnp.where(same_bin & (row % 2 > lane % 2), -1.0, other)
    real = jnp.sum(cube * first[None], axis=1)
    imag = jnp.sum(cube * other[None], axis=1)
    even = lax.broadcasted_iota(jnp.int32, (BLOCKS, width), 1) % 2 == 0
    real = real + pltpu.roll(real, width - 1, 1)
    imag = imag + pltpu.roll(imag, 1, 1)
    both = jnp.where(even, real, imag)
    left, right = both[:, :LANES], both[:, LANES:]
    left = left + pltpu.roll(left, LANES - GROUP_ROWS, 1)
    right = right + pltpu.roll(right, GROUP_ROWS, 1)
    return jnp.where(first_half((BLOCKS, LANES)), left, right)


def first_half(shape):
    return lax.broadcasted_iota(jnp.int32, shape, 1) % ROWS < GROUP_ROWS


def column_sum(value):
    return jnp.sum(value, axis=0, keepdims=True)


def leading_modes(packed, gram_ref):
    even = lax.broadcasted_iota(jnp.int32, (BLOCKS, LANES), 1) % 2 == 0
    low = first_half((BLOCKS, LANES))
    per_half = LANES // ROWS
    for half in range(2):
        if half:
            part = jnp.where(low, pltpu.roll(packed, LANES - GROUP_ROWS, 1), packed)
        else:
            part = jnp.where(low, packed, pltpu.roll(packed, GROUP_ROWS, 1))
        real = jnp.where(even, part, pltpu.roll(part, 1, 1))
        imag = jnp.where(even, pltpu.roll(part, LANES - 1, 1), part)
        for near in range(per_half):
            shift = (LANES - ROWS * near) % LANES
            block = half * per_half + near
            gram_ref[0, block] = real if shift == 0 else pltpu.roll(real, shift, 1)
            gram_ref[1, block] = imag if shift == 0 else pltpu.roll(imag, shift, 1)

    def apply_gram(vec_real, vec_imag):
        out_real = [None] * MODES
        out_imag = [None] * MODES
        for block in range(BLOCKS):
            real = gram_ref[0, block]
            imag = gram_ref[1, block]
            for j in range(MODES):
                row_real = vec_real[j][block : block + 1]
                row_imag = vec_imag[j][block : block + 1]
                term_real = real * row_real - imag * row_imag
                term_imag = real * row_imag + imag * row_real
                out_real[j] = term_real if block == 0 else out_real[j] + term_real
                out_imag[j] = term_imag if block == 0 else out_imag[j] + term_imag
        return out_real, out_imag

    def orthonormal(vec_real, vec_imag):
        vec_real = list(vec_real)
        vec_imag = list(vec_imag)
        for i in range(MODES):
            base_real = vec_real[i]
            base_imag = vec_imag[i]
            square = column_sum(base_real * base_real + base_imag * base_imag)
            inverse = 1.0 / square
            for j in range(i + 1, MODES):
                proj_real = column_sum(base_real * vec_real[j] + base_imag * vec_imag[j]) * inverse
                proj_imag = column_sum(base_real * vec_imag[j] - base_imag * vec_real[j]) * inverse
                vec_real[j] = vec_real[j] - (base_real * proj_real - base_imag * proj_imag)
                vec_imag[j] = vec_imag[j] - (base_real * proj_imag + base_imag * proj_real)
            scale = lax.rsqrt(square)
            vec_real[i] = base_real * scale
            vec_imag[i] = base_imag * scale
        return vec_real, vec_imag

    wide_real = [gram_ref[0, j] for j in range(MODES)]
    wide_imag = [gram_ref[1, j] for j in range(MODES)]
    vec_real, vec_imag = orthonormal(wide_real, wide_imag)

    def sweep(_, carry):
        return orthonormal(*apply_gram(*carry))

    vec_real, vec_imag = lax.fori_loop(1, SUBSPACE_ITERS, sweep, (vec_real, vec_imag))
    wide_real, wide_imag = apply_gram(vec_real, vec_imag)
    energies = [
        column_sum(vec_real[j] * wide_real[j] + vec_imag[j] * wide_imag[j]) for j in range(MODES)
    ]
    return vec_real, vec_imag, energies


def coefficient_matrix(vec_real, vec_imag, energies, order_ref):
    lane = lax.broadcasted_iota(jnp.int32, (BLOCKS, LANES), 1)
    even = lane % 2 == 0
    first = jnp.zeros((BLOCKS, LANES), jnp.float32)
    second = jnp.zeros((BLOCKS, LANES), jnp.float32)
    for j in range(MODES):
        scale = 1.0 / jnp.sqrt(energies[j])
        amp_real = vec_real[j] * scale
        amp_imag = vec_imag[j] * scale
        on_real = jnp.where(even, amp_real, amp_imag)
        on_imag = jnp.where(even, -amp_imag, amp_real)
        if j:
            on_real = pltpu.roll(on_real, ROWS * j, 1)
            on_imag = pltpu.roll(on_imag, ROWS * j, 1)
        here = lane // ROWS == j
        first = jnp.where(here, on_real, first)
        second = jnp.where(here, on_imag, second)
    shape = (BLOCKS, ROWS, LANES)
    row = lax.broadcasted_iota(jnp.int32, shape, 1)
    column = lax.broadcasted_iota(jnp.int32, shape, 2)
    whole = jnp.where(
        row % 2 == 0,
        jnp.broadcast_to(first[:, None, :], shape),
        jnp.broadcast_to(second[:, None, :], shape),
    )
    whole = jnp.where(row // 2 == column % ROWS // 2, whole, 0.0)
    turned = whole.reshape(BLOCKS * ROWS, LANES).T
    for j in range(MODES):
        for half in range(2):
            piece = turned[ROWS * j : ROWS * (j + 1), half * LANES : (half + 1) * LANES]
            order_ref[half, pl.ds(j, ROWS, stride=MODES), :] = piece
    ordered = [order_ref[half, : MODES * ROWS] for half in range(2)]
    return jnp.concatenate(ordered, axis=1).astype(jnp.bfloat16)


def group_modes(coef, mine_ref, columns, put):
    rows = mine_ref[:, :, columns]
    rows = rows.reshape(BLOCKS * ROWS, rows.shape[2])
    modes = jnp.dot(coef, rows, preferred_element_type=jnp.float32).astype(jnp.bfloat16)
    for half in range(GROUPS):
        for f in range(GROUP_BINS):
            for part in range(2):
                start = ((half * GROUP_BINS + f) * 2 + part) * MODES
                put(f, part, half, modes[start : start + MODES])


def spectra_kernel(
    points,
    scale,
    table_ref,
    series_ref,
    mine_ref,
    done_ref,
    coef_ref,
    energy_ref,
    rows_ref,
    round_ref,
    taken_ref,
    made_ref,
    early_ref,
    total_ref,
    packed_ref,
    gram_ref,
    order_ref,
    table_sem,
    take_sem,
    send_sem,
    recv_sem,
    sum_send_sem,
    sum_recv_sem,
    ring_sem,
    plane_sem,
):
    half_points = points // GROUPS
    made, sent = chunk_plan(points)
    lands = (early_ref, mine_ref)
    here = lax.axis_index("space")
    me = lax.axis_index("tblock")
    level = me // 2
    core = lax.rem(me, 2)
    high = here // SIDE
    wide = lax.rem(here, SIDE)

    def peer(dz, dc):
        return lax.rem(level + dz, LEVELS) * 2 + lax.rem(core + dc, 2)

    def plane(dy, dx):
        return lax.rem(high + dy, SIDE) * SIDE + lax.rem(wide + dx, SIDE)

    def signal(sem, **device):
        pl.semaphore_signal(sem, inc=1, device_id=device, device_id_type=MESH)

    rings = [[(0, 1)]] + [
        [(dz, dc) for dz in sorted({far, LEVELS - far}) for dc in (0, 1)]
        for far in range(1, LEVELS // 2 + 1)
    ]
    rings = [rings[1] + rings[0]] + rings[2:]
    peers = [pair for ring in rings[::-1] for pair in ring]

    def take(k, half):
        comp, start, width = made[k]
        return pltpu.make_async_copy(
            series_ref.at[comp, :, pl.ds(half * half_points + start, width)],
            taken_ref.at[k % 2, half, :, pl.ds(0, width)],
            take_sem.at[k % 2, half],
        )

    def send(k, dz, dc):
        group, start, width = sent[k]
        to = peer(dz, dc)
        return pltpu.make_async_remote_copy(
            src_ref=made_ref.at[group, to, :, pl.ds(start, width)],
            dst_ref=lands[group].at[me, :, pl.ds(start, width)],
            send_sem=send_sem.at[k],
            recv_sem=recv_sem.at[k],
            device_id={"tblock": to},
            device_id_type=MESH,
        )

    def whole(k):
        group, start, width = sent[k]
        part = lands[group].at[pl.ds(0, BLOCKS - 1), :, pl.ds(start, width)]
        return pltpu.make_async_remote_copy(
            src_ref=part,
            dst_ref=part,
            send_sem=send_sem.at[k],
            recv_sem=recv_sem.at[k],
            device_id={"tblock": peer(1, 0)},
            device_id_type=MESH,
        )

    def make(k):
        comp, start, width = made[k]
        columns = pl.ds(comp * half_points + start, width)
        for half in range(GROUPS):
            take(k, half).wait()
            spectra = jnp.dot(
                round_ref[...], taken_ref[k % 2, half, :, :width], preferred_element_type=jnp.float32
            )
            made_ref[:, :, pl.ds(half * GROUP_ROWS, GROUP_ROWS), columns] = spectra.astype(
                jnp.bfloat16
            ).reshape(GROUPS, BLOCKS, GROUP_ROWS, width)
            if k + 2 < len(made):
                take(k + 2, half).start()
        for group in range(GROUPS):
            lands[group][me, :, columns] = made_ref[group, me, :, columns]

    table = pltpu.make_async_copy(table_ref, rows_ref, table_sem)
    table.start()
    for half in range(GROUPS):
        take(0, half).start()
    barrier = pltpu.get_barrier_semaphore()
    for dz, dc in rings[0]:
        signal(barrier, tblock=peer(dz, dc))
    sides = [(0, 1), (0, SIDE - 1), (1, 0), (SIDE - 1, 0)]
    for dy, dx in sides:
        signal(barrier, space=plane(dy, dx))
    for half in range(GROUPS):
        take(1, half).start()
    table.wait()
    round_ref[...] = rows_ref[...].astype(jnp.bfloat16)
    make(0)
    pl.semaphore_wait(barrier, len(rings[0]) + len(sides))

    for r, ring in enumerate(rings):
        if r:
            pl.semaphore_wait(ring_sem.at[r - 1, 0], 1)
            pl.semaphore_wait(ring_sem.at[r - 1, 1], 1)
        if r + 1 < len(rings):
            signal(ring_sem.at[r, 0], tblock=peer(1, 0))
            signal(ring_sem.at[r, 1], tblock=peer(LEVELS - 1, 0))
        for dz, dc in ring:
            send(0, dz, dc).start()
        if r == 0:
            signal(plane_sem.at[0], space=plane(0, SIDE - 1))
            make(1)
        for dz, dc in ring:
            send(1, dz, dc).start()
    pl.semaphore_wait(plane_sem.at[0], 1)
    signal(plane_sem.at[1], space=plane(1, 0))
    signal(plane_sem.at[2], space=plane(SIDE - 1, 0))
    for k in range(2, len(made)):
        make(k)
    for k in range(2, len(sent)):
        for dz, dc in peers:
            send(k, dz, dc).start()
    pl.semaphore_wait(plane_sem.at[1], 1)
    pl.semaphore_wait(plane_sem.at[2], 1)
    signal(plane_sem.at[3], space=plane(SIDE - 1, 0))
    pl.semaphore_wait(plane_sem.at[3], 1)

    hops = (0, 1, 2, 1)
    others = [(dy, dx) for dy in range(SIDE) for dx in range(SIDE)][1:]
    others.sort(key=lambda step: -hops[step[0]] - hops[step[1]])

    def exchange(group, step):
        return pltpu.make_async_remote_copy(
            src_ref=packed_ref.at[group, here],
            dst_ref=packed_ref.at[group, here],
            send_sem=sum_send_sem.at[group],
            recv_sem=sum_recv_sem.at[group],
            device_id={"space": plane(*step)},
            device_id_type=MESH,
        )

    def whole_exchange(group):
        part = packed_ref.at[group, pl.ds(0, SIDE * SIDE - 1)]
        return pltpu.make_async_remote_copy(
            src_ref=part,
            dst_ref=part,
            send_sem=sum_send_sem.at[group],
            recv_sem=sum_recv_sem.at[group],
            device_id={"space": plane(0, 1)},
            device_id_type=MESH,
        )

    lane = lax.broadcasted_iota(jnp.int32, (MODES, LANES), 1)

    def gram(group):
        opened = False
        for k in range(len(sent)):
            owner, start, width = sent[k]
            if owner != group:
                continue
            whole(k).wait_recv()
            rows = lands[group][:, :, pl.ds(start, width)].reshape(BLOCKS * ROWS, width)
            part = lax.dot_general(
                rows, rows, (((1,), (1,)), ((), ())), preferred_element_type=jnp.float32
            )
            total_ref[...] = total_ref[...] + part if opened else part
            opened = True

    def settle(group, spread):
        narrow = spread
        for f in range(GROUP_BINS):
            to = group * GROUP_BINS + f
            if to != 2 * f:
                narrow = jnp.where(lane == to, pltpu.roll(spread, (to - 2 * f) % LANES, 1), narrow)
        columns = slice(group * GROUP_BINS, (group + 1) * GROUP_BINS)
        energy_ref[:, columns] = narrow[:, columns]

    def solve(group, carry):
        for fixed in range(GROUPS):

            @pl.when(group == fixed)
            def _():
                gram(fixed)

        packed_ref[group, here] = pack_gram(total_ref[...])
        for d in others:
            exchange(group, d).start()
        for fixed in range(GROUPS):

            @pl.when(group == fixed)
            def _():
                for k in range(len(sent)):
                    if sent[k][0] == fixed:
                        whole(k).wait_send()

        whole_exchange(group).wait_recv()
        packed = packed_ref[group, 0]
        for s in range(1, SIDE * SIDE):
            packed = packed + packed_ref[group, s]
        vec_real, vec_imag, energies = leading_modes(packed / scale, gram_ref)
        coef_ref[...] = coefficient_matrix(vec_real, vec_imag, energies, order_ref)
        spread = jnp.concatenate(energies, axis=0)
        whole_exchange(group).wait_send()
        for fixed in range(GROUPS):

            @pl.when(group == fixed)
            def _():
                settle(fixed, spread)

        @pl.when(group == 0)
        def _():
            for comp in range(COMPS):

                def put(f, part, half, rows):
                    done_ref[f, part, comp, :, pl.ds(half * half_points, half_points)] = rows

                columns = pl.ds(comp * half_points, half_points)
                group_modes(coef_ref[...], early_ref, columns, put)

        return carry

    lax.fori_loop(0, GROUPS, solve, 0)


def modes_kernel(
    coef_ref, mine_ref, done_ref, energy_ref, out_ref, energy_out_ref, held_ref, sem, done_sem
):
    half_points = held_ref.shape[4] // GROUPS
    first = pl.ds(0, GROUP_BINS)
    early = pltpu.make_async_copy(done_ref.at[first], out_ref.at[first], done_sem.at[0])
    early.start()
    energy = pltpu.make_async_copy(energy_ref, energy_out_ref, done_sem.at[1])
    energy.start()

    def late(comp):
        return pltpu.make_async_copy(
            held_ref.at[comp], out_ref.at[pl.ds(GROUP_BINS, GROUP_BINS), :, comp], sem.at[comp]
        )

    for comp in range(COMPS):

        def put(f, part, half, rows):
            held_ref[comp, f, part, :, pl.ds(half * half_points, half_points)] = rows

        group_modes(coef_ref[...], mine_ref, pl.ds(comp * half_points, half_points), put)
        late(comp).start()
    for comp in range(COMPS):
        late(comp).wait()
    early.wait()
    energy.wait()


def local(snapshots, space_count):
    points = snapshots.shape[3]
    width = COMPS * points // GROUPS
    pieces = len(chunk_plan(points)[1])
    series = jnp.transpose(snapshots, (0, 2, 1, 3)).reshape(COMPS, STEPS, points)
    vmem = pl.BlockSpec(memory_space=pltpu.VMEM)
    hbm = pl.BlockSpec(memory_space=pltpu.HBM)
    mine, done, coef, energies = pl.pallas_call(
        functools.partial(spectra_kernel, points, float(COMPS * points * space_count)),
        out_shape=(
            pltpu.VMEM((BLOCKS, ROWS, width), jnp.bfloat16),
            pltpu.VMEM((GROUP_BINS + 1, 2, COMPS, MODES, points), jnp.bfloat16),
            pltpu.VMEM((BINS * 2 * MODES, BLOCKS * ROWS), jnp.bfloat16),
            pltpu.VMEM((MODES, BINS), jnp.float32),
        ),
        in_specs=[hbm, hbm],
        out_specs=(vmem, vmem, vmem, vmem),
        scratch_shapes=[
            pltpu.VMEM((STEPS, STEPS), jnp.float32),
            pltpu.VMEM((STEPS, STEPS), jnp.bfloat16),
            pltpu.VMEM((2, GROUPS, STEPS, points // GROUPS), jnp.bfloat16),
            pltpu.VMEM((GROUPS, BLOCKS, ROWS, width), jnp.bfloat16),
            pltpu.VMEM((BLOCKS, ROWS, width), jnp.bfloat16),
            pltpu.VMEM((BLOCKS * ROWS, BLOCKS * ROWS), jnp.float32),
            pltpu.VMEM((GROUPS, SIDE * SIDE, BLOCKS, LANES), jnp.float32),
            pltpu.VMEM((2, BLOCKS, BLOCKS, LANES), jnp.float32),
            pltpu.VMEM((2, BINS * 2 * MODES + MARGIN, LANES), jnp.float32),
            pltpu.SemaphoreType.DMA,
            pltpu.SemaphoreType.DMA((2, GROUPS)),
            pltpu.SemaphoreType.DMA((pieces,)),
            pltpu.SemaphoreType.DMA((pieces,)),
            pltpu.SemaphoreType.DMA((GROUPS,)),
            pltpu.SemaphoreType.DMA((GROUPS,)),
            pltpu.SemaphoreType.REGULAR((LEVELS // 2 - 1, 2)),
            pltpu.SemaphoreType.REGULAR((4,)),
        ],
        compiler_params=pltpu.CompilerParams(
            collective_id=0, has_side_effects=True, vmem_limit_bytes=VMEM_BYTES
        ),
        cost_estimate=pl.CostEstimate(
            flops=4 * STEPS * STEPS * COMPS * points,
            bytes_accessed=2 * STEPS * COMPS * points,
            transcendentals=0,
        ),
        name="spectra_exchange",
    )(spectral_table(), series)
    modes, energies = pl.pallas_call(
        modes_kernel,
        out_shape=(
            jax.ShapeDtypeStruct((BINS, 2, COMPS, MODES, points), jnp.bfloat16),
            jax.ShapeDtypeStruct((MODES, BINS), jnp.float32),
        ),
        in_specs=[vmem, vmem, vmem, vmem],
        out_specs=(hbm, hbm),
        scratch_shapes=[
            pltpu.VMEM((COMPS + 1, GROUP_BINS, 2, MODES, points), jnp.bfloat16),
            pltpu.SemaphoreType.DMA((COMPS,)),
            pltpu.SemaphoreType.DMA((2,)),
        ],
        compiler_params=pltpu.CompilerParams(vmem_limit_bytes=MODES_VMEM_BYTES),
        cost_estimate=pl.CostEstimate(
            flops=4 * STEPS * BINS * 2 * MODES * COMPS * points,
            bytes_accessed=2 * STEPS * COMPS * points,
            transcendentals=0,
        ),
        name="modes_product",
    )(coef, mine, done, energies)
    return jnp.transpose(modes, (0, 1, 3, 2, 4)), energies.T


def solution(mesh):
    in_specs = (P("tblock", None, None, "space"),)
    out_specs = (P("tblock", None, None, None, "space"), P("tblock", None))
    body = functools.partial(local, space_count=mesh.shape["space"])
    return jax.shard_map(body, mesh=mesh, in_specs=in_specs, out_specs=out_specs, check_vma=False)
```

```python
import functools
import math

import jax
import jax.numpy as jnp
import numpy as np
from jax import lax
from jax.experimental import pallas as pl
from jax.experimental.pallas import tpu as pltpu
from jax.sharding import PartitionSpec as P

MODES = 4
SUBSPACE_ITERS = 6
BLOCKS = 16
STEPS = 256
BINS = 8
ROWS = 2 * BINS
COMPS = 3
GROUPS = 2
GROUP_BINS = BINS // GROUPS
GROUP_ROWS = ROWS // GROUPS
LEVELS = 8
MARGIN = 8
SIDE = 4
LANES = 128
MESH = pl.DeviceIdType.MESH
VMEM_BYTES = 50 * 2**20
MODES_VMEM_BYTES = 16 * 2**20


def spectral_table():
    times = np.arange(STEPS, dtype=np.int32)
    orders = np.arange(1, STEPS // 2 + 1, dtype=np.int32)
    phase = orders[:, None] * times[None, :] % STEPS
    angle = np.float32(2.0 * math.pi / STEPS) * phase.astype(np.float32)
    swing = np.cos(np.float32(2.0 * math.pi / STEPS) * times.astype(np.float32))
    window = np.float32(0.5) - np.float32(0.5) * swing
    scaled = window / np.float32(math.sqrt(0.375 * STEPS))
    rows = np.stack([scaled * np.cos(angle), -scaled * np.sin(angle)], axis=1)
    rows = rows.reshape(BLOCKS, GROUPS, GROUP_ROWS, STEPS).transpose(1, 0, 2, 3)
    return jnp.asarray(rows.reshape(STEPS, STEPS).astype(np.float32))


def chunk_plan(points):
    half = points // GROUPS
    first, second, last = 4 * LANES, 24 * LANES, 8 * LANES
    made = [(0, 0, first), (0, first, second - first), (0, second, half - second)]
    made += [(c, 0, half) for c in range(1, COMPS)]
    sent = [(0, 0, first), (0, first, second - first), (0, second, COMPS * half - second)]
    sent += [(1, 0, COMPS * half - last), (1, COMPS * half - last, last)]
    return made, sent


def pack_gram(total):
    width = total.shape[1]
    cube = total.reshape(BLOCKS, ROWS, width)
    row = lax.broadcasted_iota(jnp.int32, (ROWS, width), 0)
    lane = lax.broadcasted_iota(jnp.int32, (ROWS, width), 1) % ROWS
    same_bin = row // 2 == lane // 2
    same_part = row % 2 == lane % 2
    first = jnp.where(same_bin & same_part, 1.0, 0.0)
    other = jnp.where(same_bin & (row % 2 < lane % 2), 1.0, 0.0)
    other = jnp.where(same_bin & (row % 2 > lane % 2), -1.0, other)
    real = jnp.sum(cube * first[None], axis=1)
    imag = jnp.sum(cube * other[None], axis=1)
    even = lax.broadcasted_iota(jnp.int32, (BLOCKS, width), 1) % 2 == 0
    real = real + pltpu.roll(real, width - 1, 1)
    imag = imag + pltpu.roll(imag, 1, 1)
    both = jnp.where(even, real, imag)
    left, right = both[:, :LANES], both[:, LANES:]
    left = left + pltpu.roll(left, LANES - GROUP_ROWS, 1)
    right = right + pltpu.roll(right, GROUP_ROWS, 1)
    return jnp.where(first_half((BLOCKS, LANES)), left, right)


def first_half(shape):
    return lax.broadcasted_iota(jnp.int32, shape, 1) % ROWS < GROUP_ROWS


def column_sum(value):
    return jnp.sum(value, axis=0, keepdims=True)


def leading_modes(packed, gram_ref):
    even = lax.broadcasted_iota(jnp.int32, (BLOCKS, LANES), 1) % 2 == 0
    low = first_half((BLOCKS, LANES))
    per_half = LANES // ROWS
    for half in range(2):
        if half:
            part = jnp.where(low, pltpu.roll(packed, LANES - GROUP_ROWS, 1), packed)
        else:
            part = jnp.where(low, packed, pltpu.roll(packed, GROUP_ROWS, 1))
        real = jnp.where(even, part, pltpu.roll(part, 1, 1))
        imag = jnp.where(even, pltpu.roll(part, LANES - 1, 1), part)
        for near in range(per_half):
            shift = (LANES - ROWS * near) % LANES
            block = half * per_half + near
            gram_ref[0, block] = real if shift == 0 else pltpu.roll(real, shift, 1)
            gram_ref[1, block] = imag if shift == 0 else pltpu.roll(imag, shift, 1)

    def apply_gram(vec_real, vec_imag):
        out_real = [None] * MODES
        out_imag = [None] * MODES
        for block in range(BLOCKS):
            real = gram_ref[0, block]
            imag = gram_ref[1, block]
            for j in range(MODES):
                row_real = vec_real[j][block : block + 1]
                row_imag = vec_imag[j][block : block + 1]
                term_real = real * row_real - imag * row_imag
                term_imag = real * row_imag + imag * row_real
                out_real[j] = term_real if block == 0 else out_real[j] + term_real
                out_imag[j] = term_imag if block == 0 else out_imag[j] + term_imag
        return out_real, out_imag

    def orthonormal(vec_real, vec_imag):
        vec_real = list(vec_real)
        vec_imag = list(vec_imag)
        for i in range(MODES):
            base_real = vec_real[i]
            base_imag = vec_imag[i]
            square = column_sum(base_real * base_real + base_imag * base_imag)
            inverse = 1.0 / square
            for j in range(i + 1, MODES):
                proj_real = column_sum(base_real * vec_real[j] + base_imag * vec_imag[j]) * inverse
                proj_imag = column_sum(base_real * vec_imag[j] - base_imag * vec_real[j]) * inverse
                vec_real[j] = vec_real[j] - (base_real * proj_real - base_imag * proj_imag)
                vec_imag[j] = vec_imag[j] - (base_real * proj_imag + base_imag * proj_real)
            scale = lax.rsqrt(square)
            vec_real[i] = base_real * scale
            vec_imag[i] = base_imag * scale
        return vec_real, vec_imag

    wide_real = [gram_ref[0, j] for j in range(MODES)]
    wide_imag = [gram_ref[1, j] for j in range(MODES)]
    vec_real, vec_imag = orthonormal(wide_real, wide_imag)

    def sweep(_, carry):
        return orthonormal(*apply_gram(*carry))

    vec_real, vec_imag = lax.fori_loop(1, SUBSPACE_ITERS, sweep, (vec_real, vec_imag))
    wide_real, wide_imag = apply_gram(vec_real, vec_imag)
    energies = [
        column_sum(vec_real[j] * wide_real[j] + vec_imag[j] * wide_imag[j]) for j in range(MODES)
    ]
    return vec_real, vec_imag, energies


def coefficient_matrix(vec_real, vec_imag, energies, order_ref):
    lane = lax.broadcasted_iota(jnp.int32, (BLOCKS, LANES), 1)
    even = lane % 2 == 0
    first = jnp.zeros((BLOCKS, LANES), jnp.float32)
    second = jnp.zeros((BLOCKS, LANES), jnp.float32)
    for j in range(MODES):
        scale = 1.0 / jnp.sqrt(energies[j])
        amp_real = vec_real[j] * scale
        amp_imag = vec_imag[j] * scale
        on_real = jnp.where(even, amp_real, amp_imag)
        on_imag = jnp.where(even, -amp_imag, amp_real)
        if j:
            on_real = pltpu.roll(on_real, ROWS * j, 1)
            on_imag = pltpu.roll(on_imag, ROWS * j, 1)
        here = lane // ROWS == j
        first = jnp.where(here, on_real, first)
        second = jnp.where(here, on_imag, second)
    shape = (BLOCKS, ROWS, LANES)
    row = lax.broadcasted_iota(jnp.int32, shape, 1)
    column = lax.broadcasted_iota(jnp.int32, shape, 2)
    whole = jnp.where(
        row % 2 == 0,
        jnp.broadcast_to(first[:, None, :], shape),
        jnp.broadcast_to(second[:, None, :], shape),
    )
    whole = jnp.where(row // 2 == column % ROWS // 2, whole, 0.0)
    turned = whole.reshape(BLOCKS * ROWS, LANES).T
    for j in range(MODES):
        for half in range(2):
            piece = turned[ROWS * j : ROWS * (j + 1), half * LANES : (half + 1) * LANES]
            order_ref[half, pl.ds(j, ROWS, stride=MODES), :] = piece
    ordered = [order_ref[half, : MODES * ROWS] for half in range(2)]
    return jnp.concatenate(ordered, axis=1).astype(jnp.bfloat16)


def group_modes(coef, mine_ref, columns, put):
    rows = mine_ref[:, :, columns]
    rows = rows.reshape(BLOCKS * ROWS, rows.shape[2])
    modes = jnp.dot(coef, rows, preferred_element_type=jnp.float32).astype(jnp.bfloat16)
    for half in range(GROUPS):
        for f in range(GROUP_BINS):
            for part in range(2):
                start = ((half * GROUP_BINS + f) * 2 + part) * MODES
                put(f, part, half, modes[start : start + MODES])


def spectra_kernel(
    points,
    scale,
    table_ref,
    series_ref,
    mine_ref,
    done_ref,
    coef_ref,
    energy_ref,
    rows_ref,
    round_ref,
    taken_ref,
    made_ref,
    early_ref,
    total_ref,
    packed_ref,
    gram_ref,
    order_ref,
    table_sem,
    take_sem,
    send_sem,
    recv_sem,
    sum_send_sem,
    sum_recv_sem,
    ring_sem,
    plane_sem,
):
    half_points = points // GROUPS
    made, sent = chunk_plan(points)
    lands = (early_ref, mine_ref)
    here = lax.axis_index("space")
    me = lax.axis_index("tblock")
    level = me // 2
    core = lax.rem(me, 2)
    high = here // SIDE
    wide = lax.rem(here, SIDE)

    def peer(dz, dc):
        return lax.rem(level + dz, LEVELS) * 2 + lax.rem(core + dc, 2)

    def plane(dy, dx):
        return lax.rem(high + dy, SIDE) * SIDE + lax.rem(wide + dx, SIDE)

    def signal(sem, **device):
        pl.semaphore_signal(sem, inc=1, device_id=device, device_id_type=MESH)

    rings = [[(0, 1)]] + [
        [(dz, dc) for dz in sorted({far, LEVELS - far}) for dc in (0, 1)]
        for far in range(1, LEVELS // 2 + 1)
    ]
    rings = [rings[1] + rings[0]] + rings[2:]
    peers = [pair for ring in rings[::-1] for pair in ring]

    def take(k, half):
        comp, start, width = made[k]
        return pltpu.make_async_copy(
            series_ref.at[comp, :, pl.ds(half * half_points + start, width)],
            taken_ref.at[k % 2, half, :, pl.ds(0, width)],
            take_sem.at[k % 2, half],
        )

    def send(k, dz, dc):
        group, start, width = sent[k]
        to = peer(dz, dc)
        return pltpu.make_async_remote_copy(
            src_ref=made_ref.at[group, to, :, pl.ds(start, width)],
            dst_ref=lands[group].at[me, :, pl.ds(start, width)],
            send_sem=send_sem.at[k],
            recv_sem=recv_sem.at[k],
            device_id={"tblock": to},
            device_id_type=MESH,
        )

    def whole(k):
        group, start, width = sent[k]
        part = lands[group].at[pl.ds(0, BLOCKS - 1), :, pl.ds(start, width)]
        return pltpu.make_async_remote_copy(
            src_ref=part,
            dst_ref=part,
            send_sem=send_sem.at[k],
            recv_sem=recv_sem.at[k],
            device_id={"tblock": peer(1, 0)},
            device_id_type=MESH,
        )

    def make(k):
        comp, start, width = made[k]
        columns = pl.ds(comp * half_points + start, width)
        for half in range(GROUPS):
            take(k, half).wait()
            spectra = jnp.dot(
                round_ref[...], taken_ref[k % 2, half, :, :width], preferred_element_type=jnp.float32
            )
            made_ref[:, :, pl.ds(half * GROUP_ROWS, GROUP_ROWS), columns] = spectra.astype(
                jnp.bfloat16
            ).reshape(GROUPS, BLOCKS, GROUP_ROWS, width)
            if k + 2 < len(made):
                take(k + 2, half).start()
        for group in range(GROUPS):
            lands[group][me, :, columns] = made_ref[group, me, :, columns]

    table = pltpu.make_async_copy(table_ref, rows_ref, table_sem)
    table.start()
    for half in range(GROUPS):
        take(0, half).start()
    barrier = pltpu.get_barrier_semaphore()
    for dz, dc in rings[0]:
        signal(barrier, tblock=peer(dz, dc))
    sides = [(0, 1), (0, SIDE - 1), (1, 0), (SIDE - 1, 0)]
    for dy, dx in sides:
        signal(barrier, space=plane(dy, dx))
    for half in range(GROUPS):
        take(1, half).start()
    table.wait()
    round_ref[...] = rows_ref[...].astype(jnp.bfloat16)
    make(0)
    pl.semaphore_wait(barrier, len(rings[0]) + len(sides))

    for r, ring in enumerate(rings):
        if r:
            pl.semaphore_wait(ring_sem.at[r - 1, 0], 1)
            pl.semaphore_wait(ring_sem.at[r - 1, 1], 1)
        if r + 1 < len(rings):
            signal(ring_sem.at[r, 0], tblock=peer(1, 0))
            signal(ring_sem.at[r, 1], tblock=peer(LEVELS - 1, 0))
        for dz, dc in ring:
            send(0, dz, dc).start()
        if r == 0:
            signal(plane_sem.at[0], space=plane(0, SIDE - 1))
            make(1)
        for dz, dc in ring:
            send(1, dz, dc).start()
    pl.semaphore_wait(plane_sem.at[0], 1)
    signal(plane_sem.at[1], space=plane(1, 0))
    signal(plane_sem.at[2], space=plane(SIDE - 1, 0))
    for k in range(2, len(made)):
        make(k)
    for k in range(2, len(sent)):
        for dz, dc in peers:
            send(k, dz, dc).start()
    pl.semaphore_wait(plane_sem.at[1], 1)
    pl.semaphore_wait(plane_sem.at[2], 1)
    signal(plane_sem.at[3], space=plane(SIDE - 1, 0))
    pl.semaphore_wait(plane_sem.at[3], 1)

    hops = (0, 1, 2, 1)
    others = [(dy, dx) for dy in range(SIDE) for dx in range(SIDE)][1:]
    others.sort(key=lambda step: -hops[step[0]] - hops[step[1]])

    def exchange(group, step):
        return pltpu.make_async_remote_copy(
            src_ref=packed_ref.at[group, here],
            dst_ref=packed_ref.at[group, here],
            send_sem=sum_send_sem.at[group],
            recv_sem=sum_recv_sem.at[group],
            device_id={"space": plane(*step)},
            device_id_type=MESH,
        )

    def whole_exchange(group):
        part = packed_ref.at[group, pl.ds(0, SIDE * SIDE - 1)]
        return pltpu.make_async_remote_copy(
            src_ref=part,
            dst_ref=part,
            send_sem=sum_send_sem.at[group],
            recv_sem=sum_recv_sem.at[group],
            device_id={"space": plane(0, 1)},
            device_id_type=MESH,
        )

    lane = lax.broadcasted_iota(jnp.int32, (MODES, LANES), 1)

    def gram(group):
        opened = False
        for k in range(len(sent)):
            owner, start, width = sent[k]
            if owner != group:
                continue
            whole(k).wait_recv()
            rows = lands[group][:, :, pl.ds(start, width)].reshape(BLOCKS * ROWS, width)
            part = lax.dot_general(
                rows, rows, (((1,), (1,)), ((), ())), preferred_element_type=jnp.float32
            )
            total_ref[...] = total_ref[...] + part if opened else part
            opened = True

    def settle(group, spread):
        narrow = spread
        for f in range(GROUP_BINS):
            to = group * GROUP_BINS + f
            if to != 2 * f:
                narrow = jnp.where(lane == to, pltpu.roll(spread, (to - 2 * f) % LANES, 1), narrow)
        columns = slice(group * GROUP_BINS, (group + 1) * GROUP_BINS)
        energy_ref[:, columns] = narrow[:, columns]

    def solve(group, carry):
        for fixed in range(GROUPS):

            @pl.when(group == fixed)
            def _():
                gram(fixed)

        packed_ref[group, here] = pack_gram(total_ref[...])
        for d in others:
            exchange(group, d).start()
        for fixed in range(GROUPS):

            @pl.when(group == fixed)
            def _():
                for k in range(len(sent)):
                    if sent[k][0] == fixed:
                        whole(k).wait_send()

        whole_exchange(group).wait_recv()
        packed = packed_ref[group, 0]
        for s in range(1, SIDE * SIDE):
            packed = packed + packed_ref[group, s]
        vec_real, vec_imag, energies = leading_modes(packed / scale, gram_ref)
        coef_ref[...] = coefficient_matrix(vec_real, vec_imag, energies, order_ref)
        spread = jnp.concatenate(energies, axis=0)
        whole_exchange(group).wait_send()
        for fixed in range(GROUPS):

            @pl.when(group == fixed)
            def _():
                settle(fixed, spread)

        @pl.when(group == 0)
        def _():
            for comp in range(COMPS):

                def put(f, part, half, rows):
                    done_ref[f, part, comp, :, pl.ds(half * half_points, half_points)] = rows

                columns = pl.ds(comp * half_points, half_points)
                group_modes(coef_ref[...], early_ref, columns, put)

        return carry

    lax.fori_loop(0, GROUPS, solve, 0)


def modes_kernel(
    coef_ref, mine_ref, done_ref, energy_ref, out_ref, energy_out_ref, held_ref, sem, done_sem
):
    half_points = held_ref.shape[4] // GROUPS
    first = pl.ds(0, GROUP_BINS)
    early = pltpu.make_async_copy(done_ref.at[first], out_ref.at[first], done_sem.at[0])
    early.start()
    energy = pltpu.make_async_copy(energy_ref, energy_out_ref, done_sem.at[1])
    energy.start()

    def late(comp):
        return pltpu.make_async_copy(
            held_ref.at[comp], out_ref.at[pl.ds(GROUP_BINS, GROUP_BINS), :, comp], sem.at[comp]
        )

    for comp in range(COMPS):

        def put(f, part, half, rows):
            held_ref[comp, f, part, :, pl.ds(half * half_points, half_points)] = rows

        group_modes(coef_ref[...], mine_ref, pl.ds(comp * half_points, half_points), put)
        late(comp).start()
    for comp in range(COMPS):
        late(comp).wait()
    early.wait()
    energy.wait()


def local(snapshots, space_count):
    points = snapshots.shape[3]
    width = COMPS * points // GROUPS
    pieces = len(chunk_plan(points)[1])
    series = jnp.transpose(snapshots, (0, 2, 1, 3)).reshape(COMPS, STEPS, points)
    vmem = pl.BlockSpec(memory_space=pltpu.VMEM)
    hbm = pl.BlockSpec(memory_space=pltpu.HBM)
    mine, done, coef, energies = pl.pallas_call(
        functools.partial(spectra_kernel, points, float(COMPS * points * space_count)),
        out_shape=(
            pltpu.VMEM((BLOCKS, ROWS, width), jnp.bfloat16),
            pltpu.VMEM((GROUP_BINS + 1, 2, COMPS, MODES, points), jnp.bfloat16),
            pltpu.VMEM((BINS * 2 * MODES, BLOCKS * ROWS), jnp.bfloat16),
            pltpu.VMEM((MODES, BINS), jnp.float32),
        ),
        in_specs=[hbm, hbm],
        out_specs=(vmem, vmem, vmem, vmem),
        scratch_shapes=[
            pltpu.VMEM((STEPS, STEPS), jnp.float32),
            pltpu.VMEM((STEPS, STEPS), jnp.bfloat16),
            pltpu.VMEM((2, GROUPS, STEPS, points // GROUPS), jnp.bfloat16),
            pltpu.VMEM((GROUPS, BLOCKS, ROWS, width), jnp.bfloat16),
            pltpu.VMEM((BLOCKS, ROWS, width), jnp.bfloat16),
            pltpu.VMEM((BLOCKS * ROWS, BLOCKS * ROWS), jnp.float32),
            pltpu.VMEM((GROUPS, SIDE * SIDE, BLOCKS, LANES), jnp.float32),
            pltpu.VMEM((2, BLOCKS, BLOCKS, LANES), jnp.float32),
            pltpu.VMEM((2, BINS * 2 * MODES + MARGIN, LANES), jnp.float32),
            pltpu.SemaphoreType.DMA,
            pltpu.SemaphoreType.DMA((2, GROUPS)),
            pltpu.SemaphoreType.DMA((pieces,)),
            pltpu.SemaphoreType.DMA((pieces,)),
            pltpu.SemaphoreType.DMA((GROUPS,)),
            pltpu.SemaphoreType.DMA((GROUPS,)),
            pltpu.SemaphoreType.REGULAR((LEVELS // 2 - 1, 2)),
            pltpu.SemaphoreType.REGULAR((4,)),
        ],
        compiler_params=pltpu.CompilerParams(
            collective_id=0, has_side_effects=True, vmem_limit_bytes=VMEM_BYTES
        ),
        cost_estimate=pl.CostEstimate(
            flops=4 * STEPS * STEPS * COMPS * points,
            bytes_accessed=2 * STEPS * COMPS * points,
            transcendentals=0,
        ),
        name="spectra_exchange",
    )(spectral_table(), series)
    modes, energies = pl.pallas_call(
        modes_kernel,
        out_shape=(
            jax.ShapeDtypeStruct((BINS, 2, COMPS, MODES, points), jnp.bfloat16),
            jax.ShapeDtypeStruct((MODES, BINS), jnp.float32),
        ),
        in_specs=[vmem, vmem, vmem, vmem],
        out_specs=(hbm, hbm),
        scratch_shapes=[
            pltpu.VMEM((COMPS + 1, GROUP_BINS, 2, MODES, points), jnp.bfloat16),
            pltpu.SemaphoreType.DMA((COMPS,)),
            pltpu.SemaphoreType.DMA((2,)),
        ],
        compiler_params=pltpu.CompilerParams(vmem_limit_bytes=MODES_VMEM_BYTES),
        cost_estimate=pl.CostEstimate(
            flops=4 * STEPS * BINS * 2 * MODES * COMPS * points,
            bytes_accessed=2 * STEPS * COMPS * points,
            transcendentals=0,
        ),
        name="modes_product",
    )(coef, mine, done, energies)
    return jnp.transpose(modes, (0, 1, 3, 2, 4)), energies.T


def solution(mesh):
    in_specs = (P("tblock", None, None, "space"),)
    out_specs = (P("tblock", None, None, None, "space"), P("tblock", None))
    body = functools.partial(local, space_count=mesh.shape["space"])
    return jax.shard_map(body, mesh=mesh, in_specs=in_specs, out_specs=out_specs, check_vma=False)
```
